128 devices in a mesh: expert: 8 (over z, y_hi), tok: 16 (over y_lo, x, core).
Axes of the slice: x: 4, y: 4 (y_hi: 2, y_lo: 2; y = y_hi * 2 + y_lo), z: 4, core: 2. Of those that a mesh axis runs over, the one named last changes fastest.
Arguments:
- x_in: bfloat16 [2048, 8192], P('tok', 'expert'), may hold values from -6 to 6
- conv_w: float32 [4, 8192], P(None, 'expert'), may hold values from -3 to 3
- b_proj: bfloat16 [2048, 128], P('tok'), may hold values from -0.0234375 to 0.0234375
- c_proj: bfloat16 [2048, 128], P('tok'), may hold values from -6 to 6
- log_decay: float32 [2048, 128], P('tok', 'expert'), may hold values from -1 to 0
- d_skip: float32 [128], P('expert'), may hold values from 0.5 to 1.5
- w_out: bfloat16 [8192, 4096], P('expert', 'tok'), may hold values from -0.0625 to 0.0625
- norm_gain: float32 [4096], replicated, may hold values from 0.5 to 2
- w_router: bfloat16 [4096, 8], replicated, may hold values from -0.09375 to 0.09375
- w_expert: bfloat16 [8, 3, 4096, 12288], P('expert', None, None, 'tok'), may hold values from -0.09375 to 0.09375
- route_ids: int32 [16, 128, 2], P('tok', 'expert'), may hold values from 0 to 7, as said below
Outputs:
- layer_out: bfloat16 [16, 128, 4096], P('tok', 'expert')
The draws below stay inside these ranges and needn't reach their ends.
Inputs may be any that keep to these rules, and one draw needn't show every extreme that they name: `route_ids`: each row names two different experts. Among the 16 rows that one device holds, one expert, the same on every device, is named by exactly 10 rows, and every other expert by at most 4 rows; some expert other than that one reaches 4 on every device.
All inputs are finite; a program needn't handle non-finite values.
Results may differ from the reference program's by a relative error of at most 0.034.
Values may be sent and summed in bfloat16 or wider, within the bound.
A program may use at most 192 MiB of HBM per device.

```python
import math
import jax
import jax.numpy as jnp
from jax import lax

D = 4096
TOP = 2
N_STATE = 128
CONV = 4
CH = 8192
HEAD = 64
FF = 12288
BLOCK = 128
SEQ_DEV = 128
STEP_COUNT = 2048
SHARDS = 16
EXPERTS = 8
RECURRENT_LANES = 128
M_TOK = 16
HOT_MOST = 10
N_TOK = 16


def draw_log_decay(key, part):
    sampler_seeds = jax.random.split(key, 6)
    slow_share = 0.5
    is_slow = jax.random.uniform(sampler_seeds[0], (RECURRENT_LANES,)) < slow_share
    slow_rate = jnp.exp(jax.random.uniform(sampler_seeds[1], (RECURRENT_LANES,), minval=math.log(0.05), maxval=0.0)) / STEP_COUNT
    fast_rate = jnp.exp(jax.random.uniform(sampler_seeds[2], (RECURRENT_LANES,), minval=math.log(1.0 / 50.0), maxval=math.log(1.0 / 20.0)))
    fading_rate = jnp.where(is_slow, slow_rate, fast_rate)
    scaling_factor = jax.random.uniform(sampler_seeds[3], (STEP_COUNT, RECURRENT_LANES), minval=0.5, maxval=1.5)
    spike_onset = (jax.random.uniform(sampler_seeds[4], (STEP_COUNT, 1)) < 2.0 / STEP_COUNT).astype(jnp.float32)
    spike_extent = jax.random.uniform(sampler_seeds[5], (STEP_COUNT, RECURRENT_LANES), minval=0.22, maxval=0.69) * spike_onset
    return (-(fading_rate[None, :] * scaling_factor) - spike_extent).astype(jnp.float32)


def draw_route_ids(key, part):
    hot_key, block_key = jax.random.split(key)
    hot_expert = jax.random.randint(hot_key, (), 0, EXPERTS).astype(jnp.int32)
    block_count = STEP_COUNT // M_TOK

    def one_block(block_sub):
        sampler_seeds = jax.random.split(block_sub, 4)
        shuffled = jax.random.permutation(sampler_seeds[0], M_TOK).astype(jnp.int32)
        takes_hot = shuffled < HOT_MOST
        needed = 2 - takes_hot.astype(jnp.int32)
        start_slot = jnp.cumsum(needed) - needed
        others = jax.random.permutation(sampler_seeds[1], EXPERTS - 1).astype(jnp.int32)
        offset = jax.random.randint(sampler_seeds[2], (), 0, EXPERTS - 1).astype(jnp.int32)

        def expert_at(slot_index):
            other_id = others[(slot_index + offset) % (EXPERTS - 1)]
            return other_id + (other_id >= hot_expert).astype(jnp.int32)
        first_pick = jnp.where(takes_hot, hot_expert, expert_at(start_slot))
        second_pick = jnp.where(takes_hot, expert_at(start_slot), expert_at(start_slot + 1))
        swapped = jax.random.randint(sampler_seeds[3], (M_TOK,), 0, 2) == 1
        return jnp.stack([jnp.where(swapped, second_pick, first_pick), jnp.where(swapped, first_pick, second_pick)], axis=-1)
    blocks_out = jax.vmap(one_block)(jax.random.split(block_key, block_count))
    return blocks_out.reshape(SHARDS, SEQ_DEV, TOP).astype(jnp.int32)


def level_of(own_key, extent, pieces, smallest, top_value):
    loudness = 1.0
    for dim, blocks in pieces:
        draws = jax.random.uniform(jax.random.fold_in(jax.random.fold_in(own_key, 6), dim), (blocks,), jnp.float32, smallest / len(pieces), top_value / len(pieces))
        loudness = loudness * jnp.repeat(jnp.exp(draws), extent[dim] // blocks).reshape((-1,) + (1,) * (len(extent) - 1 - dim))
    return loudness


def scatter_about(key, shape, scale, most, cuts=(), kind=jnp.bfloat16):
    factor_of = level_of(key, shape, cuts, -0.22, 0.18) if cuts else 1.0
    array = jax.random.normal(key, shape, jnp.float32) * scale * factor_of
    return jnp.minimum(jnp.maximum(array, -most), most).astype(kind)


def setup_inputs(seed: int = 0) -> dict:
    arg_keys = jax.random.split(jax.random.key(seed), 12)
    return {
        "x_in": scatter_about(arg_keys[0], (STEP_COUNT, CH), 1.0, 6.0, ((0, 16), (1, 8))),
        "conv_w": scatter_about(arg_keys[1], (CONV, CH), CONV ** -0.5, 3.0, ((1, 8),), jnp.float32),
        "b_proj": scatter_about(arg_keys[2], (STEP_COUNT, N_STATE), (N_STATE * STEP_COUNT // 4) ** -0.5, 0.0234375, ((0, 16),)),
        "c_proj": scatter_about(arg_keys[3], (STEP_COUNT, N_STATE), 1.0, 6.0, ((0, 16),)),
        "log_decay": draw_log_decay(jax.random.fold_in(arg_keys[11], 71), 0),
        "d_skip": jnp.clip(0.5 + 1.0 * jax.random.uniform(arg_keys[5], (RECURRENT_LANES,), jnp.float32) ** level_of(arg_keys[5], (RECURRENT_LANES,), ((0, 8),), -0.2, 0.2), 0.5, 1.5),
        "w_out": scatter_about(arg_keys[6], (CH, D), CH ** -0.5, 0.0625, ((0, 8), (1, 16))),
        "norm_gain": jnp.clip(jnp.exp(jax.random.uniform(arg_keys[7], (D,), jnp.float32, math.log(0.5), math.log(2.0))), 0.5, 2.0),
        "w_router": scatter_about(arg_keys[8], (D, EXPERTS), D ** -0.5, 0.09375),
        "w_expert": scatter_about(arg_keys[9], (EXPERTS, 3, D, FF), D ** -0.5, 0.09375, ((0, 8), (3, 16))),
        "route_ids": draw_route_ids(jax.random.fold_in(arg_keys[11], 71), 0),
    }


highest = lax.Precision.HIGHEST

def block_terms(x_block, b_block, c_block, decay_block):
    length = decay_block.shape[0]
    cumulative = jnp.cumsum(decay_block, axis=0).T
    spread = cumulative[:, :, None] - cumulative[:, None, :]
    lower_mask = jnp.arange(length, dtype=jnp.int32)[:, None] >= jnp.arange(length, dtype=jnp.int32)[None, :]
    decay_matrix = jnp.where(lower_mask[None], jnp.exp(jnp.where(lower_mask[None], spread, 0.0)), 0.0)
    scores = jnp.einsum('in,jn->ij', c_block, b_block, precision=highest)
    y_local = jnp.einsum('hij,jhp->ihp', decay_matrix * scores[None], x_block, precision=highest)
    tail_decay = jnp.exp(cumulative[:, -1:] - cumulative)
    state_block = jnp.einsum('hj,jhp,jn->hpn', tail_decay, x_block, b_block, precision=highest)
    total_decay = jnp.exp(cumulative[:, -1])
    entry_decay = jnp.exp(cumulative)
    return (y_local, state_block, total_decay, entry_decay)

def reference(x_in, conv_w, b_proj, c_proj, log_decay, d_skip, w_out, norm_gain, w_router, w_expert, route_ids):
    padded = jnp.concatenate([jnp.zeros((CONV - 1, CH), jnp.float32), x_in.astype(jnp.float32)], axis=0)
    conv_sum = conv_w[0] * padded[0:STEP_COUNT]
    for offset in range(1, CONV):
        conv_sum = conv_sum + conv_w[offset] * padded[offset:offset + STEP_COUNT]
    conv_out = jax.nn.silu(conv_sum)
    blocks = STEP_COUNT // BLOCK
    x_heads = conv_out.reshape(blocks, BLOCK, RECURRENT_LANES, HEAD)
    b_blocks = b_proj.astype(jnp.float32).reshape(blocks, BLOCK, N_STATE)
    c_blocks = c_proj.astype(jnp.float32).reshape(blocks, BLOCK, N_STATE)
    decay_blocks = log_decay.reshape(blocks, BLOCK, RECURRENT_LANES)

    def block_step(state, inputs):
        y_local, state_block, total_decay, entry_decay = block_terms(*inputs)
        y_carry = jnp.einsum('hi,in,hpn->ihp', entry_decay, inputs[2], state, precision=highest)
        new_state = total_decay[:, None, None] * state + state_block
        return (new_state, y_local + y_carry)
    start_state = jnp.zeros((RECURRENT_LANES, HEAD, N_STATE), jnp.float32)
    _, y_blocks = lax.scan(block_step, start_state, (x_heads, b_blocks, c_blocks, decay_blocks))
    mixed = y_blocks.reshape(STEP_COUNT, RECURRENT_LANES, HEAD) + d_skip[None, :, None] * conv_out.reshape(STEP_COUNT, RECURRENT_LANES, HEAD)
    scan_out = mixed.reshape(STEP_COUNT, CH).astype(jnp.bfloat16)
    hidden = jnp.dot(scan_out, w_out, preferred_element_type=jnp.float32).astype(jnp.bfloat16)
    hidden_f = hidden.astype(jnp.float32)
    mean_square = lax.optimization_barrier(jnp.mean(hidden_f * hidden_f, axis=-1, keepdims=True))
    normed = (hidden_f * lax.rsqrt(mean_square + 1e-05) * norm_gain).astype(jnp.bfloat16)
    logits = jnp.dot(normed, w_router, preferred_element_type=jnp.float32)
    route = route_ids.reshape(STEP_COUNT, TOP).astype(jnp.int32)
    picked = jnp.take_along_axis(logits, route, axis=1)
    sigmas = jax.nn.sigmoid(picked)
    gates = sigmas / lax.optimization_barrier(jnp.sum(sigmas, axis=1, keepdims=True))
    pair_expert = route.reshape(-1)
    pair_gate = gates.reshape(-1)
    slice_width = FF // N_TOK
    limit = STEP_COUNT
    group_rows = math.gcd(512, limit)
    groups_per = limit // group_rows

    def positions_of(expert):
        found = jnp.nonzero(pair_expert == expert, size=limit, fill_value=2 * STEP_COUNT)[0]
        return found.astype(jnp.int32)
    positions = jax.vmap(positions_of)(jnp.arange(EXPERTS, dtype=jnp.int32))

    def add_group(step_index, total):
        expert = (step_index // groups_per).astype(jnp.int32)
        group = (step_index % groups_per).astype(jnp.int32)
        chosen = lax.dynamic_slice_in_dim(positions[expert], group * group_rows, group_rows, 0)
        present = chosen < 2 * STEP_COUNT

        def compute(running):
            token_index = jnp.minimum(chosen // 2, STEP_COUNT - 1).astype(jnp.int32)
            gathered = normed[token_index]
            weights = w_expert[expert]
            gate_value = jnp.dot(gathered, weights[0], preferred_element_type=jnp.float32)
            up_value = jnp.dot(gathered, weights[1], preferred_element_type=jnp.float32)
            active = (jax.nn.silu(gate_value) * up_value).astype(jnp.bfloat16)
            result = jnp.zeros((group_rows, D), jnp.float32)
            for part_index in range(N_TOK):
                first_unit = part_index * slice_width
                piece = lax.dot_general(active[:, first_unit:first_unit + slice_width], weights[2][:, first_unit:first_unit + slice_width], (((1,), (1,)), ((), ())), preferred_element_type=jnp.float32)
                result = result + lax.optimization_barrier(piece.astype(jnp.bfloat16)).astype(jnp.float32)
            weight_row = jnp.where(present, pair_gate[jnp.minimum(chosen, 2 * STEP_COUNT - 1)], 0.0)
            return running.at[token_index].add(result * weight_row[:, None])
        return lax.cond(present[0], compute, lambda running: running, total)
    moe = lax.fori_loop(0, EXPERTS * groups_per, add_group, jnp.zeros((STEP_COUNT, D), jnp.float32))
    layer_out = (hidden_f + moe).astype(jnp.bfloat16)
    return layer_out.reshape(SHARDS, SEQ_DEV, D)
```

```python
import jax
import jax.numpy as jnp
from jax import lax
from jax.experimental import pallas as pl
from jax.experimental.pallas import tpu as pltpu
from jax.sharding import PartitionSpec as P

N_STATE = 128
CONV = 4
HEAD = 64
BLOCK = 128


highest = lax.Precision.HIGHEST


def from_behind(value, axis, steps):
    count = lax.axis_size(axis)
    first, last = (max(0, -steps), min(count, count - steps))
    return lax.ppermute(value, axis, [(source, source + steps) for source in range(first, last)])


def prefix_state(decay, state, axis):
    heads, head, n = state.shape
    packed = jnp.concatenate(
        [state, jnp.broadcast_to(decay[:, None, None], (heads, 8, n))], axis=1
    ).astype(jnp.bfloat16)
    gathered = lax.all_gather(packed, axis)
    place = lax.axis_index(axis)

    def one(step, held):
        item = lax.dynamic_index_in_dim(gathered, step, 0, False).astype(jnp.float32)
        return item[:, head : head + 1] * held + item[:, :head]

    return lax.fori_loop(0, place, one, jnp.zeros_like(state))


def block_terms(x_block, b_block, c_block, decay_block):
    length = decay_block.shape[0]
    ones = jnp.tril(jnp.ones((length, length), jnp.float32))
    cumulative = jnp.einsum("ij,jh->hi", ones, decay_block, precision=highest)
    spread = cumulative[:, :, None] - cumulative[:, None, :]
    lower_mask = (
        jnp.arange(length, dtype=jnp.int32)[:, None] >= jnp.arange(length, dtype=jnp.int32)[None, :]
    )
    decay_matrix = jnp.where(
        lower_mask[None], jnp.exp(jnp.where(lower_mask[None], spread, 0.0)), 0.0
    )
    scores = jnp.einsum("in,jn->ij", c_block, b_block, precision=highest)
    y_local = jnp.einsum("hij,jhp->ihp", decay_matrix * scores[None], x_block, precision=highest)
    tail_decay = jnp.exp(cumulative[:, -1:] - cumulative)
    state_block = jnp.einsum("hj,jhp,jn->hpn", tail_decay, x_block, b_block, precision=highest)
    total_decay = jnp.exp(cumulative[:, -1])
    entry_decay = jnp.exp(cumulative)
    return (y_local, state_block, total_decay, entry_decay)


MESH = pl.DeviceIdType.MESH
bf16, f32 = jnp.bfloat16, jnp.float32
NX, NE = 4, 8
ORDER = [(0, 0), (0, 1), (1, 0), (3, 0), (2, 0), (2, 1), (1, 1), (3, 1)]
PLACE = {d: i for i, d in enumerate(ORDER)}


def slot(dx, dy, dc):
    return PLACE[(dx % NX, dy % 2)] * 2 + dc % 2


class Where:
    def __init__(self):
        self.e = lax.axis_index("expert")
        self.t = lax.axis_index("tok")
        self.c = lax.rem(self.t, 2)
        self.x = lax.rem(self.t // 2, NX)
        self.y = self.t // (2 * NX)

    def tok(self, dx, dy, dc):
        return (
            lax.rem(self.y + dy, 2) * NX + lax.rem(self.x + dx, NX)
        ) * 2 + lax.rem(self.c + dc, 2)

    def tok_dev(self, dx, dy, dc):
        return {"tok": self.tok(dx, dy, dc)}

    def exp(self, k):
        return lax.rem(self.e + k, NE)


NEAR = [(0, 0, 1), (0, 1, 0), (1, 0, 0), (3, 0, 0), (2, 0, 0)]


def greet(w):
    barrier = pltpu.get_barrier_semaphore()
    for d in NEAR:
        pl.semaphore_signal(barrier, inc=1, device_id=w.tok_dev(*d), device_id_type=MESH)
    for k in range(1, NE):
        pl.semaphore_signal(barrier, inc=1, device_id={"expert": w.exp(k)}, device_id_type=MESH)
    pl.semaphore_wait(barrier, len(NEAR) + NE - 1)


class Mail:
    def __init__(self, sems):
        self.sems, self.out = sems, []

    def send(self, src, dst, rsem, dev):
        cp = pltpu.make_async_remote_copy(
            src_ref=src, dst_ref=dst, send_sem=self.sems.at[len(self.out)], recv_sem=rsem,
            device_id=dev, device_id_type=MESH,
        )
        cp.start()
        self.out.append(cp)

    def got(self, ref, rsem, dev):
        pltpu.make_async_remote_copy(
            src_ref=ref, dst_ref=ref, send_sem=self.sems.at[0], recv_sem=rsem,
            device_id=dev, device_id_type=MESH,
        ).wait_recv()

    def drain(self):
        for cp in self.out:
            cp.wait_send()


class Gather:
    def __init__(self, w, mail, view, rsems):
        self.w, self.mail, self.view, self.rsems = w, mail, view, rsems

    def put(self, frm, part, to, seen):
        s = slot(*seen)
        self.mail.send(
            self.view(slot(*frm), part), self.view(s, part), self.rsems.at[s, part],
            self.w.tok_dev(*to),
        )

    def got(self, dx, dy, dc, part):
        s = slot(dx, dy, dc)
        self.mail.got(self.view(s, part), self.rsems.at[s, part], self.w.tok_dev(0, 0, 1))

    def start(self):
        own = (0, 0, 0)
        for part in (1, 0):
            self.put(own, part, (0, 1, 0), (0, 1, 0))
        for dx in (1, 3, 2):
            self.put(own, 0, (dx, 0, 0), (-dx, 0, 0))
        for dx in (1, 3, 2):
            self.put(own, 1, (dx, 0, 0), (-dx, 0, 0))
        for part in (0, 1):
            self.put(own, part, (0, 0, 1), (0, 0, 1))

    def sib(self, dx, dy, part):
        self.put((dx, dy, 0), part, (0, 0, 1), (dx, dy, 1))

    def y_in(self):
        self.got(0, 1, 0, 1)
        for dx in (1, 3, 2):
            self.put((0, 1, 0), 1, (dx, 0, 0), (-dx, 1, 0))
        self.sib(0, 1, 1)
        self.got(0, 1, 0, 0)
        self.sib(0, 1, 0)

    def x_in(self, dx):
        self.got(dx, 0, 0, 0)
        self.put((dx, 0, 0), 0, (0, 1, 0), (dx, 1, 0))
        self.sib(dx, 0, 0)

    def x_in_late(self, dx):
        self.got(dx, 0, 0, 1)
        self.sib(dx, 0, 1)

    def far_in(self, dx):
        for part in (0, 1):
            self.got(dx, 1, 0, part)
            self.sib(dx, 1, part)

    def sib_in(self, dx, dy):
        for part in (0, 1):
            self.got(dx, dy, 1, part)


AG_SENDS = 2 + 3 + 3 + 2 + (3 + 2) + 3 * 2 + 3 + 3 * 2


def rms(hid, gain):
    ms = jnp.mean(hid * hid, axis=-1, keepdims=True)
    return hid * lax.rsqrt(ms + 1e-05) * gain


def project_kernel(
    scan_ref, wout_ref, gain_ref, hid_ref, nrm_ref, g_ref, part_ref, rec_ref, ssem, rsem, esem
):
    w = Where()
    mail = Mail(ssem)
    depth = wout_ref.shape[0]
    cut = depth * 5 // 8
    greet(w)

    def view(s, part):
        return g_ref.at[s, pl.ds(0, cut)] if part == 0 else g_ref.at[s, pl.ds(cut, depth - cut)]

    g_ref[0] = wout_ref[...]
    ag = Gather(w, mail, view, rsem)
    ag.start()
    width = wout_ref.shape[1]

    def mult(dx, dy, dc):
        cols = pl.ds(pl.multiple_of(w.tok(dx, dy, dc) * width, width), width)
        part_ref[:, cols] = jnp.dot(
            scan_ref[...], g_ref[slot(dx, dy, dc)], preferred_element_type=f32
        ).astype(bf16)

    mult(0, 0, 0)
    ag.y_in()
    for dx in (1, 3, 2):
        ag.x_in(dx)
    ag.sib_in(0, 0)
    mult(0, 0, 1)
    mult(0, 1, 0)
    for dx in (1, 3, 2):
        ag.x_in_late(dx)
        mult(dx, 0, 0)
    ag.sib_in(0, 1)
    mult(0, 1, 1)
    for dx in (1, 3, 2):
        ag.far_in(dx)
        mult(dx, 1, 0)
    for dy in (0, 1):
        for dx in (1, 3, 2):
            ag.sib_in(dx, dy)
            mult(dx, dy, 1)
    rows = hid_ref.shape[0]

    def mine(e):
        return pl.ds(pl.multiple_of(e * rows, rows), rows)

    for k in range(1, NE):
        mail.send(
            part_ref.at[mine(w.exp(k))], rec_ref.at[k - 1], esem.at[k - 1], {"expert": w.exp(k)}
        )
    total = part_ref[mine(w.e), :].astype(f32)
    for k in range(1, NE):
        mail.got(rec_ref.at[k - 1], esem.at[k - 1], {"expert": w.exp(k)})
        total = total + rec_ref[k - 1].astype(f32)
    hid_b = total.astype(bf16)
    hid_ref[...] = hid_b
    nrm_ref[...] = rms(hid_b.astype(f32), gain_ref[...]).astype(bf16)
    mail.drain()


def project(scan_out, w_out, gain, rows):
    depth, width = w_out.shape
    toks, model = scan_out.shape[0], gain.shape[1]
    vm = pl.BlockSpec(memory_space=pltpu.VMEM)
    return pl.pallas_call(
        project_kernel,
        out_shape=[jax.ShapeDtypeStruct((rows, model), bf16)] * 2,
        in_specs=[vm] * 3,
        out_specs=[vm] * 2,
        scratch_shapes=[
            pltpu.VMEM((16, depth, width), bf16),
            pltpu.VMEM((toks, model), bf16),
            pltpu.VMEM((NE - 1, rows, model), bf16),
            pltpu.SemaphoreType.DMA((AG_SENDS + NE - 1,)),
            pltpu.SemaphoreType.DMA((16, 2)),
            pltpu.SemaphoreType.DMA((NE - 1,)),
        ],
        compiler_params=pltpu.CompilerParams(
            collective_id=1, has_side_effects=True, vmem_limit_bytes=40 * 2**20
        ),
        cost_estimate=pl.CostEstimate(
            flops=2 * toks * depth * model, bytes_accessed=20 * 2**20, transcendentals=0
        ),
        name="project",
    )(scan_out, w_out, gain)


def expert_kernel(
    nrm_ref, rt_ref, hid_ref, wr_ref, we_ref, out_ref,
    wv_ref, n_ref, r_ref, g_ref, a_ref, o_ref, sib_ref, yp_ref, yq_ref, xp_ref, xq_ref,
    con_ref, rec_ref,
    lsem, ssem, nsem, tsem, gsem, bsem, psem, qsem, fsem, esem,
):
    w = Where()
    mail = Mail(ssem)
    rows, model = nrm_ref.shape
    cap = g_ref.shape[1]
    hidden = wv_ref.shape[2]
    toks = n_ref.shape[0]
    cut = model * 5 // 8
    P, Q = pl.ds(0, cut), pl.ds(cut, model - cut)
    loads = [pltpu.make_async_copy(we_ref.at[0, i], wv_ref.at[i], lsem.at[i]) for i in range(3)]
    for cp in loads:
        cp.start()
    greet(w)

    def of(e):
        return pl.ds(pl.multiple_of(e * rows, rows), rows)

    me = of(w.e)
    for k in range(1, NE):
        mail.send(rt_ref, r_ref.at[me], tsem.at[k - 1], {"expert": w.exp(k)})
        mail.send(nrm_ref, n_ref.at[me], nsem.at[k - 1], {"expert": w.exp(k)})
    n_ref[me, :] = nrm_ref[...]
    r_ref[me, :] = rt_ref[...]
    for k in range(1, NE):
        frm = of(w.exp(NE - k))
        mail.got(r_ref.at[frm], tsem.at[k - 1], {"expert": w.exp(k)})
        mail.got(n_ref.at[frm], nsem.at[k - 1], {"expert": w.exp(k)})

    ii = lax.broadcasted_iota(jnp.int32, (toks, toks), 0)
    jj = lax.broadcasted_iota(jnp.int32, (toks, toks), 1)
    eye = (ii == jj).astype(f32)
    r1 = r_ref[:, 0:1].astype(f32)
    r2 = r_ref[:, 1:2].astype(f32)
    e_f = w.e.astype(f32)
    hit = jnp.where(r1 == e_f, 1.0, 0.0) + jnp.where(r2 == e_f, 1.0, 0.0)
    rank = jnp.sum(jnp.where(ii < jj, hit, 0.0), axis=0, keepdims=True)
    hit_row = jnp.sum(hit * eye, axis=0, keepdims=True)
    want = lax.broadcasted_iota(jnp.int32, (cap, toks), 0).astype(f32)
    sel_f = jnp.where(want == rank, 1.0, 0.0) * hit_row
    sel = sel_f.astype(bf16)
    for b in range(4):
        cols = pl.ds(b * (model // 4), model // 4)
        g_ref[0, :, cols] = jnp.dot(sel, n_ref[:, cols], preferred_element_type=f32).astype(bf16)

    def view(s, part):
        return g_ref.at[s, :, Q if part else P]

    ag = Gather(w, mail, view, gsem)
    ag.start()

    logits = jnp.dot(n_ref[...], wr_ref[...], preferred_element_type=f32)
    lane = lax.broadcasted_iota(jnp.int32, logits.shape, 1).astype(f32)
    s1 = jax.nn.sigmoid(jnp.sum(jnp.where(lane == r1, logits, 0.0), axis=1, keepdims=True))
    s2 = jax.nn.sigmoid(jnp.sum(jnp.where(lane == r2, logits, 0.0), axis=1, keepdims=True))
    gate = jnp.where(r1 == e_f, s1, s2) / (s1 + s2)
    gate_row = jnp.sum(gate * eye, axis=0, keepdims=True)
    gate_col = jnp.sum(sel_f * gate_row, axis=1, keepdims=True)

    def compute(group):
        xs = pl.ds(group * 4, 4)
        tile = 256

        @pl.loop(0, hidden // tile)
        def _(i):
            cols = pl.ds(pl.multiple_of(i * tile, tile), tile)
            xg = g_ref[xs].reshape(4 * cap, model)
            gv = jnp.dot(xg, wv_ref[0, :, cols], preferred_element_type=f32)
            uv = jnp.dot(xg, wv_ref[1, :, cols], preferred_element_type=f32)
            a_ref[:, cols] = (gv / (1.0 + jnp.exp(-gv)) * uv).astype(bf16)

        if group == 0:
            loads[2].wait()

        @pl.loop(0, model // tile)
        def _(i):
            cols = pl.ds(pl.multiple_of(i * tile, tile), tile)
            o = lax.dot_general(
                a_ref[...], wv_ref[2, cols, :], (((1,), (1,)), ((), ())), preferred_element_type=f32
            )
            o_ref[xs, :, cols] = o.astype(bf16).reshape(4, cap, tile)

    def add(dst, cols, *srcs):
        @pl.loop(0, cap // 16)
        def _(i):
            r = pl.ds(pl.multiple_of(i * 16, 16), 16)
            v = o_ref[dst, r, cols].astype(f32)
            for src in srcs:
                v = v + src(r).astype(f32)
            o_ref[dst, r, cols] = v.astype(bf16)

    def pair_out(group):
        for p in (0, 1):
            i = group * 2 + p
            mail.send(o_ref.at[i * 2 + 1], sib_ref.at[i], bsem.at[i], w.tok_dev(0, 0, 1))

    def pair_in(group):
        for p in (0, 1):
            i = group * 2 + p
            dx, dy = ORDER[i]
            mail.got(sib_ref.at[i], bsem.at[i], w.tok_dev(0, 0, 1))
            add(i * 2, slice(None), lambda r, i=i: sib_ref[i, r, :])
            if dy == 1:
                mail.send(o_ref.at[i * 2, :, P], yp_ref.at[dx], psem.at[dx], w.tok_dev(0, 1, 0))
            if dx != 0:
                b = (NX - dx - 1) * 2 + dy
                mail.send(o_ref.at[i * 2, :, Q], xq_ref.at[b], qsem.at[b], w.tok_dev(dx, 0, 0))

    def y_sum(dx):
        mail.got(yp_ref.at[dx], psem.at[dx], w.tok_dev(0, 1, 0))
        add(slot(dx, 0, 0), P, lambda r: yp_ref[dx, r, :])
        if dx != 0:
            b = NX - dx - 1
            mail.send(o_ref.at[slot(dx, 0, 0), :, P], xp_ref.at[b], fsem.at[b], w.tok_dev(dx, 0, 0))

    def x_sum(dy):
        for b in range(3):
            mail.got(xq_ref.at[b * 2 + dy], qsem.at[b * 2 + dy], w.tok_dev(1, 0, 0))
        add(slot(0, dy, 0), Q, *[lambda r, b=b: xq_ref[b * 2 + dy, r, :] for b in range(3)])
        if dy == 1:
            mail.send(o_ref.at[slot(0, 1, 0), :, Q], yq_ref, fsem.at[3], w.tok_dev(0, 1, 0))

    ag.y_in()
    ag.sib_in(0, 0)
    ag.sib_in(0, 1)
    loads[0].wait()
    loads[1].wait()
    compute(0)
    pair_out(0)
    for dx in (1, 3, 2):
        ag.x_in(dx)
    for dx in (1, 3):
        ag.x_in_late(dx)
    ag.x_in_late(2)
    ag.sib_in(1, 0)
    ag.sib_in(3, 0)
    compute(1)
    pair_out(1)
    for dx in (2, 1, 3):
        ag.far_in(dx)
    pair_in(0)
    ag.sib_in(2, 0)
    ag.sib_in(2, 1)
    compute(2)
    pair_out(2)
    pair_in(1)
    ag.sib_in(1, 1)
    ag.sib_in(3, 1)
    compute(3)
    pair_out(3)
    pair_in(2)
    y_sum(2)
    pair_in(3)
    y_sum(1)
    y_sum(3)
    x_sum(1)
    y_sum(0)
    x_sum(0)

    for b in range(3):
        mail.got(xp_ref.at[b], fsem.at[b], w.tok_dev(1, 0, 0))
    mail.got(yq_ref, fsem.at[3], w.tok_dev(0, 1, 0))

    def final(cols, srcs):
        v = o_ref[0, :, cols].astype(f32)
        for src in srcs:
            v = v + src.astype(f32)
        return lax.dot_general(
            sel, (v * gate_col).astype(bf16), (((0,), (0,)), ((), ())), preferred_element_type=f32
        ).astype(bf16)

    con_ref[:, P] = final(P, [xp_ref[b] for b in range(3)])
    con_ref[:, Q] = final(Q, [yq_ref[...]])
    for k in range(1, NE):
        mail.send(con_ref.at[of(w.exp(k))], rec_ref.at[k - 1], esem.at[k - 1], {"expert": w.exp(k)})
    total = hid_ref[...].astype(f32) + con_ref[me, :].astype(f32)
    for k in range(1, NE):
        mail.got(rec_ref.at[k - 1], esem.at[k - 1], {"expert": w.exp(k)})
        total = total + rec_ref[k - 1].astype(f32)
    out_ref[...] = total.astype(bf16)
    mail.drain()


def expert_layer(normed, route, hidden, w_router, w_expert):
    rows, model = normed.shape
    units = w_expert.shape[3]
    toks, cap = rows * NE, 80
    cut = model * 5 // 8
    vm = pl.BlockSpec(memory_space=pltpu.VMEM)
    sends = 2 * (NE - 1) + AG_SENDS + 8 + 4 + 6 + 3 + 1 + NE - 1
    dma = pltpu.SemaphoreType.DMA
    return pl.pallas_call(
        expert_kernel,
        out_shape=jax.ShapeDtypeStruct((rows, model), bf16),
        in_specs=[vm] * 4 + [pl.BlockSpec(memory_space=pl.ANY)],
        out_specs=vm,
        scratch_shapes=[
            pltpu.VMEM((3, model, units), bf16),
            pltpu.VMEM((toks, model), bf16),
            pltpu.VMEM((toks, 128), bf16),
            pltpu.VMEM((16, cap, model), bf16),
            pltpu.VMEM((4 * cap, units), bf16),
            pltpu.VMEM((16, cap, model), bf16),
            pltpu.VMEM((8, cap, model), bf16),
            pltpu.VMEM((4, cap, cut), bf16),
            pltpu.VMEM((cap, model - cut), bf16),
            pltpu.VMEM((3, cap, cut), bf16),
            pltpu.VMEM((6, cap, model - cut), bf16),
            pltpu.VMEM((toks, model), bf16),
            pltpu.VMEM((NE - 1, rows, model), bf16),
            dma((3,)), dma((sends,)), dma((NE - 1,)), dma((NE - 1,)), dma((16, 2)), dma((8,)),
            dma((4,)), dma((6,)), dma((4,)), dma((NE - 1,)),
        ],
        compiler_params=pltpu.CompilerParams(
            collective_id=2, has_side_effects=True, vmem_limit_bytes=60 * 2**20
        ),
        cost_estimate=pl.CostEstimate(
            flops=6 * 16 * cap * model * units, bytes_accessed=20 * 2**20, transcendentals=0
        ),
        name="expert_layer",
    )(normed, route, hidden, w_router, w_expert)


def on_device(
    x_in, conv_w, b_proj, c_proj, log_decay, d_skip, w_out, norm_gain, w_router, w_expert, route_ids
):
    seq_rows, chan_dev = x_in.shape
    tail_rows = x_in[seq_rows - (CONV - 1) :]
    earlier_rows = from_behind(tail_rows, "tok", 1)
    extended = jnp.concatenate([earlier_rows, x_in], axis=0).astype(jnp.float32)
    conv_sum = conv_w[0] * extended[0:seq_rows]
    for offset in range(1, CONV):
        conv_sum = conv_sum + conv_w[offset] * extended[offset : offset + seq_rows]
    conv_out = jax.nn.silu(conv_sum)
    heads_dev = chan_dev // HEAD
    blocks = seq_rows // BLOCK
    x_heads = conv_out.reshape(blocks, BLOCK, heads_dev, HEAD)
    b_blocks = b_proj.astype(jnp.float32).reshape(blocks, BLOCK, N_STATE)
    c_blocks = c_proj.astype(jnp.float32).reshape(blocks, BLOCK, N_STATE)
    decay_blocks = log_decay.reshape(blocks, BLOCK, heads_dev)

    def local_step(carry_pair, inputs):
        carry_decay, carry_state = carry_pair
        y_local, state_block, total_decay, entry_decay = block_terms(*inputs)
        advanced = (
            carry_decay * total_decay,
            total_decay[:, None, None] * carry_state + state_block,
        )
        return (advanced, (y_local, entry_decay, carry_decay, carry_state))

    identity = (
        jnp.ones((heads_dev,), jnp.float32),
        jnp.zeros((heads_dev, HEAD, N_STATE), jnp.float32),
    )
    device_total, stacked = lax.scan(
        local_step, identity, (x_heads, b_blocks, c_blocks, decay_blocks)
    )
    y_locals, entry_decays, lead_decays, lead_states = stacked
    prefix = prefix_state(*device_total, "tok")
    incoming = lead_decays[:, :, None, None] * prefix[None] + lead_states
    y_carry = jnp.einsum("bhi,bin,bhpn->bihp", entry_decays, c_blocks, incoming, precision=highest)
    mixed = (y_locals + y_carry).reshape(seq_rows, heads_dev, HEAD) + d_skip[
        None, :, None
    ] * conv_out.reshape(seq_rows, heads_dev, HEAD)
    scan_out = mixed.reshape(seq_rows, chan_dev).astype(jnp.bfloat16)
    rows, model = route_ids.shape[1], norm_gain.shape[0]
    route = jnp.pad(route_ids[0].astype(jnp.bfloat16), ((0, 0), (0, 126)))
    hidden, normed = project(scan_out, w_out, norm_gain[None], rows)
    layer_out = expert_layer(normed, route, hidden, w_router, w_expert)
    return layer_out.reshape(1, rows, model)


def solution(mesh):
    placed = (
        P("tok", "expert"),
        P(None, "expert"),
        P("tok", None),
        P("tok", None),
        P("tok", "expert"),
        P("expert"),
        P("expert", "tok"),
        P(),
        P(),
        P("expert", None, None, "tok"),
        P("tok", "expert", None),
    )
    return jax.shard_map(
        on_device, mesh=mesh, in_specs=placed, out_specs=P("tok", "expert", None), check_vma=False
    )
```

```python
import jax
import jax.numpy as jnp
from jax import lax
from jax.experimental import pallas as pl
from jax.experimental.pallas import tpu as pltpu
from jax.sharding import PartitionSpec as P

CONV = 4
HEAD = 64
highest = lax.Precision.HIGHEST
MESH = pl.DeviceIdType.MESH
bf16, f32 = jnp.bfloat16, jnp.float32
NX, NE = 4, 8
ORDER = [(0, 0), (0, 1), (1, 0), (3, 0), (2, 0), (2, 1), (1, 1), (3, 1)]
PLACE = {d: i for i, d in enumerate(ORDER)}


def slot(dx, dy, dc):
    return PLACE[(dx % NX, dy % 2)] * 2 + dc % 2


class Where:
    def __init__(self):
        self.e = lax.axis_index("expert")
        self.t = lax.axis_index("tok")
        self.c = lax.rem(self.t, 2)
        self.x = lax.rem(self.t // 2, NX)
        self.y = self.t // (2 * NX)

    def tok(self, dx, dy, dc):
        return (
            lax.rem(self.y + dy, 2) * NX + lax.rem(self.x + dx, NX)
        ) * 2 + lax.rem(self.c + dc, 2)

    def tok_dev(self, dx, dy, dc):
        return {"tok": self.tok(dx, dy, dc)}

    def exp(self, k):
        return lax.rem(self.e + k, NE)


NEAR = [(0, 0, 1), (0, 1, 0), (1, 0, 0), (3, 0, 0), (2, 0, 0)]


def greet(w, behind=False):
    barrier = pltpu.get_barrier_semaphore()
    for d in NEAR:
        pl.semaphore_signal(barrier, inc=1, device_id=w.tok_dev(*d), device_id_type=MESH)
    for k in range(1, NE):
        pl.semaphore_signal(barrier, inc=1, device_id={"expert": w.exp(k)}, device_id_type=MESH)
    if behind:
        back = lax.rem(w.t + 4 * NX - 1, 4 * NX)
        pl.semaphore_signal(barrier, inc=1, device_id={"tok": back}, device_id_type=MESH)
    pl.semaphore_wait(barrier, len(NEAR) + NE - 1 + behind)


class Mail:
    def __init__(self, sems):
        self.sems, self.out = sems, []

    def send(self, src, dst, rsem, dev):
        cp = pltpu.make_async_remote_copy(
            src_ref=src, dst_ref=dst, send_sem=self.sems.at[len(self.out)], recv_sem=rsem,
            device_id=dev, device_id_type=MESH,
        )
        cp.start()
        self.out.append(cp)

    def got(self, ref, rsem, dev):
        pltpu.make_async_remote_copy(
            src_ref=ref, dst_ref=ref, send_sem=self.sems.at[0], recv_sem=rsem,
            device_id=dev, device_id_type=MESH,
        ).wait_recv()

    def drain(self):
        for cp in self.out:
            cp.wait_send()


class Gather:
    def __init__(self, w, mail, view, rsems):
        self.w, self.mail, self.view, self.rsems = w, mail, view, rsems

    def put(self, frm, part, to, seen):
        s = slot(*seen)
        self.mail.send(
            self.view(slot(*frm), part), self.view(s, part), self.rsems.at[s, part],
            self.w.tok_dev(*to),
        )

    def got(self, dx, dy, dc, part):
        s = slot(dx, dy, dc)
        self.mail.got(self.view(s, part), self.rsems.at[s, part], self.w.tok_dev(0, 0, 1))

    def start(self):
        own = (0, 0, 0)
        for part in (1, 0):
            self.put(own, part, (0, 1, 0), (0, 1, 0))
        for dx in (1, 3, 2):
            self.put(own, 0, (dx, 0, 0), (-dx, 0, 0))
        for dx in (1, 3, 2):
            self.put(own, 1, (dx, 0, 0), (-dx, 0, 0))
        for part in (0, 1):
            self.put(own, part, (0, 0, 1), (0, 0, 1))

    def sib(self, dx, dy, part):
        self.put((dx, dy, 0), part, (0, 0, 1), (dx, dy, 1))

    def y_in(self):
        self.got(0, 1, 0, 1)
        for dx in (1, 3, 2):
            self.put((0, 1, 0), 1, (dx, 0, 0), (-dx, 1, 0))
        self.sib(0, 1, 1)
        self.got(0, 1, 0, 0)
        self.sib(0, 1, 0)

    def x_in(self, dx):
        self.got(dx, 0, 0, 0)
        self.put((dx, 0, 0), 0, (0, 1, 0), (dx, 1, 0))
        self.sib(dx, 0, 0)

    def x_in_late(self, dx):
        self.got(dx, 0, 0, 1)
        self.sib(dx, 0, 1)

    def far_in(self, dx):
        for part in (0, 1):
            self.got(dx, 1, 0, part)
            self.sib(dx, 1, part)

    def sib_in(self, dx, dy):
        for part in (0, 1):
            self.got(dx, dy, 1, part)


AG_SENDS = 2 + 3 + 3 + 2 + (3 + 2) + 3 * 2 + 3 + 3 * 2


def rms(hid, gain):
    ms = jnp.mean(hid * hid, axis=-1, keepdims=True)
    return hid * lax.rsqrt(ms + 1e-05) * gain


def mixer_kernel(
    x_ref, cw_ref, b_ref, c_ref, ld_ref, ds_ref, wout_ref, gain_ref,
    hid_ref, nrm_ref,
    g_ref, part_ref, rec_ref, ext_ref, tail_ref, conv_ref, y_ref, ent_ref, st_ref, s1_ref, s2_ref,
    r_in_ref, r_out_ref, sin_ref, hand_ref, scan_ref,
    ssem, rsem, esem, tsem, usem,
):
    w = Where()
    mail = Mail(ssem)
    toks, chans = x_ref.shape
    heads = ld_ref.shape[1]
    half = chans // 2
    n_state = b_ref.shape[1]
    depth, width = wout_ref.shape
    cut = depth * 5 // 8
    sib = w.tok_dev(0, 0, 1)
    greet(w, behind=True)
    mail.send(
        x_ref.at[pl.ds(toks - 16, 16)], tail_ref, tsem.at[0], {"tok": lax.rem(w.t + 1, 4 * NX)}
    )

    def view(s, part):
        return g_ref.at[s, pl.ds(0, cut)] if part == 0 else g_ref.at[s, pl.ds(cut, depth - cut)]

    g_ref[0] = wout_ref[...]
    ag = Gather(w, mail, view, rsem)
    ag.start()

    ext_ref[16:, :] = x_ref[...].astype(f32)
    mail.got(tail_ref, tsem.at[0], sib)
    ext_ref[0:16, :] = jnp.where(w.t > 0, tail_ref[...].astype(f32), 0.0)
    for b in range(chans // 256):
        cols = pl.ds(b * 256, 256)
        v = cw_ref[0:1, cols] * ext_ref[13 : 13 + toks, cols]
        for k in range(1, CONV):
            v = v + cw_ref[k : k + 1, cols] * ext_ref[13 + k : 13 + k + toks, cols]
        conv_ref[:, cols] = v / (1.0 + jnp.exp(-v))

    ii = lax.broadcasted_iota(jnp.int32, (toks, toks), 0)
    jj = lax.broadcasted_iota(jnp.int32, (toks, toks), 1)
    low = ii >= jj
    lowf = jnp.where(low, 1.0, 0.0)
    cum = jnp.dot(lowf, ld_ref[...], precision=highest, preferred_element_type=f32)
    cum_t = lax.dot_general(
        ld_ref[...], jnp.where(ii <= jj, 1.0, 0.0), (((0,), (0,)), ((), ())),
        precision=highest, preferred_element_type=f32,
    )
    eh = lax.broadcasted_iota(jnp.int32, (heads, chans), 0) * HEAD
    ec = lax.broadcasted_iota(jnp.int32, (heads, chans), 1)
    spread = jnp.where((ec >= eh) & (ec < eh + HEAD), 1.0, 0.0)
    both = jnp.concatenate([cum, cum[toks - 1 : toks] - cum], axis=0)
    skip = jnp.dot(ds_ref[...], spread, precision=highest, preferred_element_type=f32)
    for h in range(2):
        for b in range(2):
            cols = pl.ds(h * half + b * (half // 2), half // 2)
            here = pl.ds(b * (half // 2), half // 2)
            sp = spread[:, h * half + b * (half // 2) : h * half + (b + 1) * (half // 2)]
            lev = jnp.exp(jnp.dot(both, sp, precision=highest, preferred_element_type=f32))
            ent_ref[:, cols] = lev[:toks]
            total = lev[toks - 1 : toks]
            xw = (conv_ref[:, cols] * lev[toks:]).astype(bf16)
            st_ref[h, 0:n_state, here] = lax.dot_general(
                b_ref[...], xw, (((0,), (0,)), ((), ())), preferred_element_type=f32
            ).astype(bf16)
            hi = total.astype(bf16).astype(f32)
            row = lax.broadcasted_iota(jnp.int32, (16, half // 2), 0)
            st_ref[h, n_state : n_state + 16, here] = jnp.where(row == 0, hi, total - hi).astype(bf16)

    mail.send(st_ref.at[1 - w.c], s1_ref, usem.at[0], sib)

    scores = lax.dot_general(
        c_ref[...], b_ref[...], (((1,), (1,)), ((), ())), preferred_element_type=f32
    )
    scores = jnp.where(low, scores, 0.0)
    lane = lax.broadcasted_iota(jnp.int32, (toks, 2 * HEAD), 1)

    def inside(p):
        cols = pl.ds(p * 2 * HEAD, 2 * HEAD)
        xc = conv_ref[:, cols]
        mats = []
        for h in (2 * p, 2 * p + 1):
            gap = jnp.where(low, cum[:, h : h + 1] - cum_t[h : h + 1, :], 0.0)
            mats.append((jnp.exp(gap) * scores).astype(bf16))
        yy = jnp.dot(jnp.concatenate(mats, axis=0), xc.astype(bf16), preferred_element_type=f32)
        y_ref[:, cols] = (
            jnp.where(lane < HEAD, yy[:toks], yy[toks:])
            + skip[:, p * 2 * HEAD : (p + 1) * 2 * HEAD] * xc
        )

    for p in range(2):
        inside(p)

    def by_rows(body):
        @pl.loop(0, n_state // 16)
        def _(i):
            body(pl.ds(pl.multiple_of(i * 16, 16), 16))

    def decay_of(block):
        v = block.astype(f32)
        return v[0:1] + v[1:2]

    DEC = pl.ds(n_state, 16)
    mail.got(s1_ref, usem.at[0], sib)
    own_d = decay_of(st_ref[w.c, DEC, :])
    sib_d = decay_of(s1_ref[DEC, :])
    first = w.c == 0
    d0 = jnp.where(first, own_d, sib_d)
    d1 = jnp.where(first, sib_d, own_d)
    chip_d = d0 * d1
    chip_hi = chip_d.astype(bf16).astype(f32)
    row = lax.broadcasted_iota(jnp.int32, (16, half), 0)
    s2_ref[w.x, DEC, :] = jnp.where(row == 0, chip_hi, chip_d - chip_hi).astype(bf16)

    def join(r):
        own, other = st_ref[w.c, r, :].astype(f32), s1_ref[r, :].astype(f32)
        s2_ref[w.x, r, :] = (
            d1 * jnp.where(first, own, other) + jnp.where(first, other, own)
        ).astype(bf16)

    by_rows(join)
    for i, dx in enumerate((1, 3, 2)):
        mail.send(s2_ref.at[w.x], s2_ref.at[w.x], tsem.at[1 + NX - dx], w.tok_dev(dx, 0, 0))
    for p in range(2, 5):
        inside(p)
    ag.y_in()
    for p in range(5, heads // 2):
        inside(p)
    for dx in (1, 3, 2):
        mail.got(s2_ref.at[lax.rem(w.x + dx, NX)], tsem.at[1 + dx], w.tok_dev(dx, 0, 0))
    decs = [decay_of(s2_ref[k, DEC, :]) for k in range(NX)]
    before_d = jnp.ones_like(chip_d)
    for k in range(NX):
        before_d = before_d * jnp.where(w.x > k, decs[k], 1.0)

    def row_scan(r):
        run = jnp.zeros((16, half), f32)
        before = run
        for k in range(NX):
            before = jnp.where(w.x == k, run, before)
            run = decs[k] * run + s2_ref[k, r, :].astype(f32)
        r_out_ref[0, r, :] = run.astype(bf16)
        r_out_ref[1, r, :] = before.astype(bf16)

    by_rows(row_scan)
    mail.send(r_out_ref.at[0], r_in_ref, usem.at[1], w.tok_dev(0, 1, 0))
    for dx in (1, 3, 2):
        ag.x_in(dx)
    mail.got(r_in_ref, usem.at[1], w.tok_dev(0, 1, 0))
    lower = w.y > 0

    def enter(r):
        chip = r_out_ref[1, r, :].astype(f32) + jnp.where(
            lower, before_d * r_in_ref[r, :].astype(f32), 0.0
        )
        s0 = jnp.where(first, st_ref[w.c, r, :], s1_ref[r, :]).astype(f32)
        second = d0 * chip + s0
        sin_ref[w.c, r, :] = jnp.where(first, chip, second).astype(bf16)
        hand_ref[r, :] = jnp.where(first, second, chip).astype(bf16)

    by_rows(enter)
    mail.send(hand_ref, sin_ref.at[w.c], usem.at[2], sib)

    def close(h):
        for b in range(2):
            cols = pl.ds(pl.multiple_of(h * half + b * (half // 2), half // 2), half // 2)
            here = pl.ds(b * (half // 2), half // 2)
            carry = jnp.dot(c_ref[...], sin_ref[h, :, here], preferred_element_type=f32)
            scan_ref[:, cols] = (y_ref[:, cols] + ent_ref[:, cols] * carry).astype(bf16)

    close(w.c)
    mail.got(sin_ref.at[1 - w.c], usem.at[2], sib)
    close(1 - w.c)

    def mult(dx, dy, dc):
        cols = pl.ds(pl.multiple_of(w.tok(dx, dy, dc) * width, width), width)
        part_ref[:, cols] = jnp.dot(
            scan_ref[...], g_ref[slot(dx, dy, dc)], preferred_element_type=f32
        ).astype(bf16)

    for dx in (1, 3, 2):
        ag.x_in_late(dx)
    mult(0, 0, 0)
    ag.sib_in(0, 0)
    mult(0, 0, 1)
    mult(0, 1, 0)
    ag.sib_in(0, 1)
    mult(0, 1, 1)
    for dx in (1, 3, 2):
        mult(dx, 0, 0)
        ag.sib_in(dx, 0)
        mult(dx, 0, 1)
    for dx in (1, 3, 2):
        ag.far_in(dx)
        mult(dx, 1, 0)
    for dx in (1, 3, 2):
        ag.sib_in(dx, 1)
        mult(dx, 1, 1)
    rows = hid_ref.shape[0]

    def mine(e):
        return pl.ds(pl.multiple_of(e * rows, rows), rows)

    for k in range(1, NE):
        mail.send(
            part_ref.at[mine(w.exp(k))], rec_ref.at[k - 1], esem.at[k - 1], {"expert": w.exp(k)}
        )
    total = part_ref[mine(w.e), :].astype(f32)
    for k in range(1, NE):
        mail.got(rec_ref.at[k - 1], esem.at[k - 1], {"expert": w.exp(k)})
        total = total + rec_ref[k - 1].astype(f32)
    hid_b = total.astype(bf16)
    hid_ref[...] = hid_b
    nrm_ref[...] = rms(hid_b.astype(f32), gain_ref[...]).astype(bf16)
    mail.drain()


def mixer(x_in, conv_w, b_proj, c_proj, log_decay, d_skip, w_out, gain, rows):
    depth, width = w_out.shape
    toks, chans = x_in.shape
    model, n_state = gain.shape[1], b_proj.shape[1]
    half = chans // 2
    vm = pl.BlockSpec(memory_space=pltpu.VMEM)
    dma = pltpu.SemaphoreType.DMA
    return pl.pallas_call(
        mixer_kernel,
        out_shape=[jax.ShapeDtypeStruct((rows, model), bf16)] * 2,
        in_specs=[vm] * 8,
        out_specs=[vm] * 2,
        scratch_shapes=[
            pltpu.VMEM((16, depth, width), bf16),
            pltpu.VMEM((toks, model), bf16),
            pltpu.VMEM((NE - 1, rows, model), bf16),
            pltpu.VMEM((toks + 16, chans), f32),
            pltpu.VMEM((16, chans), bf16),
            pltpu.VMEM((toks, chans), f32),
            pltpu.VMEM((toks, chans), f32),
            pltpu.VMEM((toks, chans), f32),
            pltpu.VMEM((2, n_state + 16, half), bf16),
            pltpu.VMEM((n_state + 16, half), bf16),
            pltpu.VMEM((NX, n_state + 16, half), bf16),
            pltpu.VMEM((n_state, half), bf16),
            pltpu.VMEM((2, n_state, half), bf16),
            pltpu.VMEM((2, n_state, half), bf16),
            pltpu.VMEM((n_state, half), bf16),
            pltpu.VMEM((toks, chans), bf16),
            dma((AG_SENDS + NE - 1 + 7,)),
            dma((16, 2)),
            dma((NE - 1,)),
            dma((1 + NX,)),
            dma((3,)),
        ],
        compiler_params=pltpu.CompilerParams(
            collective_id=1, has_side_effects=True, vmem_limit_bytes=40 * 2**20
        ),
        cost_estimate=pl.CostEstimate(
            flops=2 * toks * depth * model, bytes_accessed=20 * 2**20, transcendentals=0
        ),
        name="mixer",
    )(x_in, conv_w, b_proj, c_proj, log_decay, d_skip, w_out, gain)


def expert_kernel(
    nrm_ref, rt_ref, hid_ref, wr_ref, we_ref, out_ref,
    wv_ref, n_ref, r_ref, g_ref, a_ref, o_ref, sib_ref, yp_ref, yq_ref, xp_ref, xq_ref,
    con_ref, rec_ref,
    lsem, ssem, nsem, tsem, gsem, bsem, psem, qsem, fsem, esem,
):
    w = Where()
    mail = Mail(ssem)
    rows, model = nrm_ref.shape
    cap = g_ref.shape[1]
    hidden = wv_ref.shape[2]
    toks = n_ref.shape[0]
    cut = model * 5 // 8
    P, Q = pl.ds(0, cut), pl.ds(cut, model - cut)
    loads = [pltpu.make_async_copy(we_ref.at[0, i], wv_ref.at[i], lsem.at[i]) for i in range(3)]
    for cp in loads:
        cp.start()
    greet(w)

    def of(e):
        return pl.ds(pl.multiple_of(e * rows, rows), rows)

    me = of(w.e)
    for k in range(1, NE):
        mail.send(rt_ref, r_ref.at[me], tsem.at[k - 1], {"expert": w.exp(k)})
        mail.send(nrm_ref, n_ref.at[me], nsem.at[k - 1], {"expert": w.exp(k)})
    n_ref[me, :] = nrm_ref[...]
    r_ref[me, :] = rt_ref[...]
    for k in range(1, NE):
        frm = of(w.exp(NE - k))
        mail.got(r_ref.at[frm], tsem.at[k - 1], {"expert": w.exp(k)})
        mail.got(n_ref.at[frm], nsem.at[k - 1], {"expert": w.exp(k)})

    ii = lax.broadcasted_iota(jnp.int32, (toks, toks), 0)
    jj = lax.broadcasted_iota(jnp.int32, (toks, toks), 1)
    eye = (ii == jj).astype(f32)
    r1 = r_ref[:, 0:1].astype(f32)
    r2 = r_ref[:, 1:2].astype(f32)
    e_f = w.e.astype(f32)
    hit = jnp.where(r1 == e_f, 1.0, 0.0) + jnp.where(r2 == e_f, 1.0, 0.0)
    rank = jnp.sum(jnp.where(ii < jj, hit, 0.0), axis=0, keepdims=True)
    hit_row = jnp.sum(hit * eye, axis=0, keepdims=True)
    want = lax.broadcasted_iota(jnp.int32, (cap, toks), 0).astype(f32)
    sel_f = jnp.where(want == rank, 1.0, 0.0) * hit_row
    sel = sel_f.astype(bf16)
    for b in range(4):
        cols = pl.ds(b * (model // 4), model // 4)
        g_ref[0, :, cols] = jnp.dot(sel, n_ref[:, cols], preferred_element_type=f32).astype(bf16)

    def view(s, part):
        return g_ref.at[s, :, Q if part else P]

    ag = Gather(w, mail, view, gsem)
    ag.start()

    logits = jnp.dot(n_ref[...], wr_ref[...], preferred_element_type=f32)
    lane = lax.broadcasted_iota(jnp.int32, logits.shape, 1).astype(f32)
    s1 = jax.nn.sigmoid(jnp.sum(jnp.where(lane == r1, logits, 0.0), axis=1, keepdims=True))
    s2 = jax.nn.sigmoid(jnp.sum(jnp.where(lane == r2, logits, 0.0), axis=1, keepdims=True))
    gate = jnp.where(r1 == e_f, s1, s2) / (s1 + s2)
    gate_row = jnp.sum(gate * eye, axis=0, keepdims=True)
    gate_col = jnp.sum(sel_f * gate_row, axis=1, keepdims=True)

    def compute(group):
        xs = pl.ds(group * 4, 4)
        tile = 256

        @pl.loop(0, hidden // tile)
        def _(i):
            cols = pl.ds(pl.multiple_of(i * tile, tile), tile)
            xg = g_ref[xs].reshape(4 * cap, model)
            gv = jnp.dot(xg, wv_ref[0, :, cols], preferred_element_type=f32)
            uv = jnp.dot(xg, wv_ref[1, :, cols], preferred_element_type=f32)
            a_ref[:, cols] = (gv / (1.0 + jnp.exp(-gv)) * uv).astype(bf16)

        if group == 0:
            loads[2].wait()

        @pl.loop(0, model // tile)
        def _(i):
            cols = pl.ds(pl.multiple_of(i * tile, tile), tile)
            o = lax.dot_general(
                a_ref[...], wv_ref[2, cols, :], (((1,), (1,)), ((), ())), preferred_element_type=f32
            )
            o_ref[xs, :, cols] = o.astype(bf16).reshape(4, cap, tile)

    def add(dst, cols, *srcs):
        @pl.loop(0, cap // 16)
        def _(i):
            r = pl.ds(pl.multiple_of(i * 16, 16), 16)
            v = o_ref[dst, r, cols].astype(f32)
            for src in srcs:
                v = v + src(r).astype(f32)
            o_ref[dst, r, cols] = v.astype(bf16)

    def pair_out(group):
        for p in (0, 1):
            i = group * 2 + p
            mail.send(o_ref.at[i * 2 + 1], sib_ref.at[i], bsem.at[i], w.tok_dev(0, 0, 1))

    def pair_in(group):
        for p in (0, 1):
            i = group * 2 + p
            dx, dy = ORDER[i]
            mail.got(sib_ref.at[i], bsem.at[i], w.tok_dev(0, 0, 1))
            add(i * 2, slice(None), lambda r, i=i: sib_ref[i, r, :])
            if dy == 1:
                mail.send(o_ref.at[i * 2, :, P], yp_ref.at[dx], psem.at[dx], w.tok_dev(0, 1, 0))
            if dx != 0:
                b = (NX - dx - 1) * 2 + dy
                mail.send(o_ref.at[i * 2, :, Q], xq_ref.at[b], qsem.at[b], w.tok_dev(dx, 0, 0))

    def y_sum(dx):
        mail.got(yp_ref.at[dx], psem.at[dx], w.tok_dev(0, 1, 0))
        add(slot(dx, 0, 0), P, lambda r: yp_ref[dx, r, :])
        if dx != 0:
            b = NX - dx - 1
            mail.send(o_ref.at[slot(dx, 0, 0), :, P], xp_ref.at[b], fsem.at[b], w.tok_dev(dx, 0, 0))

    def x_sum(dy):
        for b in range(3):
            mail.got(xq_ref.at[b * 2 + dy], qsem.at[b * 2 + dy], w.tok_dev(1, 0, 0))
        add(slot(0, dy, 0), Q, *[lambda r, b=b: xq_ref[b * 2 + dy, r, :] for b in range(3)])
        if dy == 1:
            mail.send(o_ref.at[slot(0, 1, 0), :, Q], yq_ref, fsem.at[3], w.tok_dev(0, 1, 0))

    ag.y_in()
    ag.sib_in(0, 0)
    ag.sib_in(0, 1)
    loads[0].wait()
    loads[1].wait()
    compute(0)
    pair_out(0)
    for dx in (1, 3, 2):
        ag.x_in(dx)
    for dx in (1, 3):
        ag.x_in_late(dx)
    ag.x_in_late(2)
    ag.sib_in(1, 0)
    ag.sib_in(3, 0)
    compute(1)
    pair_out(1)
    for dx in (2, 1, 3):
        ag.far_in(dx)
    pair_in(0)
    ag.sib_in(2, 0)
    ag.sib_in(2, 1)
    compute(2)
    pair_out(2)
    pair_in(1)
    ag.sib_in(1, 1)
    ag.sib_in(3, 1)
    compute(3)
    pair_out(3)
    pair_in(2)
    y_sum(2)
    pair_in(3)
    y_sum(1)
    y_sum(3)
    x_sum(1)
    y_sum(0)
    x_sum(0)

    for b in range(3):
        mail.got(xp_ref.at[b], fsem.at[b], w.tok_dev(1, 0, 0))
    mail.got(yq_ref, fsem.at[3], w.tok_dev(0, 1, 0))

    def final(cols, srcs):
        v = o_ref[0, :, cols].astype(f32)
        for src in srcs:
            v = v + src.astype(f32)
        return lax.dot_general(
            sel, (v * gate_col).astype(bf16), (((0,), (0,)), ((), ())), preferred_element_type=f32
        ).astype(bf16)

    con_ref[:, P] = final(P, [xp_ref[b] for b in range(3)])
    con_ref[:, Q] = final(Q, [yq_ref[...]])
    for k in range(1, NE):
        mail.send(con_ref.at[of(w.exp(k))], rec_ref.at[k - 1], esem.at[k - 1], {"expert": w.exp(k)})
    total = hid_ref[...].astype(f32) + con_ref[me, :].astype(f32)
    for k in range(1, NE):
        mail.got(rec_ref.at[k - 1], esem.at[k - 1], {"expert": w.exp(k)})
        total = total + rec_ref[k - 1].astype(f32)
    out_ref[...] = total.astype(bf16)
    mail.drain()


def expert_layer(normed, route, hidden, w_router, w_expert):
    rows, model = normed.shape
    units = w_expert.shape[3]
    toks, cap = rows * NE, 80
    cut = model * 5 // 8
    vm = pl.BlockSpec(memory_space=pltpu.VMEM)
    sends = 2 * (NE - 1) + AG_SENDS + 8 + 4 + 6 + 3 + 1 + NE - 1
    dma = pltpu.SemaphoreType.DMA
    return pl.pallas_call(
        expert_kernel,
        out_shape=jax.ShapeDtypeStruct((rows, model), bf16),
        in_specs=[vm] * 4 + [pl.BlockSpec(memory_space=pl.ANY)],
        out_specs=vm,
        scratch_shapes=[
            pltpu.VMEM((3, model, units), bf16),
            pltpu.VMEM((toks, model), bf16),
            pltpu.VMEM((toks, 128), bf16),
            pltpu.VMEM((16, cap, model), bf16),
            pltpu.VMEM((4 * cap, units), bf16),
            pltpu.VMEM((16, cap, model), bf16),
            pltpu.VMEM((8, cap, model), bf16),
            pltpu.VMEM((4, cap, cut), bf16),
            pltpu.VMEM((cap, model - cut), bf16),
            pltpu.VMEM((3, cap, cut), bf16),
            pltpu.VMEM((6, cap, model - cut), bf16),
            pltpu.VMEM((toks, model), bf16),
            pltpu.VMEM((NE - 1, rows, model), bf16),
            dma((3,)), dma((sends,)), dma((NE - 1,)), dma((NE - 1,)), dma((16, 2)), dma((8,)),
            dma((4,)), dma((6,)), dma((4,)), dma((NE - 1,)),
        ],
        compiler_params=pltpu.CompilerParams(
            collective_id=2, has_side_effects=True, vmem_limit_bytes=60 * 2**20
        ),
        cost_estimate=pl.CostEstimate(
            flops=6 * 16 * cap * model * units, bytes_accessed=20 * 2**20, transcendentals=0
        ),
        name="expert_layer",
    )(normed, route, hidden, w_router, w_expert)


def on_device(
    x_in, conv_w, b_proj, c_proj, log_decay, d_skip, w_out, norm_gain, w_router, w_expert, route_ids
):
    rows, model = route_ids.shape[1], norm_gain.shape[0]
    route = jnp.pad(route_ids[0].astype(bf16), ((0, 0), (0, 126)))
    hidden, normed = mixer(
        x_in, conv_w, b_proj, c_proj, log_decay, d_skip[None], w_out, norm_gain[None], rows
    )
    layer_out = expert_layer(normed, route, hidden, w_router, w_expert)
    return layer_out.reshape(1, rows, model)


def solution(mesh):
    placed = (
        P("tok", "expert"),
        P(None, "expert"),
        P("tok", None),
        P("tok", None),
        P("tok", "expert"),
        P("expert"),
        P("expert", "tok"),
        P(),
        P(),
        P("expert", None, None, "tok"),
        P("tok", "expert", None),
    )
    return jax.shard_map(
        on_device, mesh=mesh, in_specs=placed, out_specs=P("tok", "expert", None), check_vma=False
    )
```

```python
import jax
import jax.numpy as jnp
from jax import lax
from jax.experimental import pallas as pl
from jax.experimental.pallas import tpu as pltpu
from jax.sharding import PartitionSpec as P

CONV = 4
HEAD = 64
highest = lax.Precision.HIGHEST
MESH = pl.DeviceIdType.MESH
bf16, f32 = jnp.bfloat16, jnp.float32
NX, NE = 4, 8
ORDER = [(0, 0), (0, 1), (1, 0), (3, 0), (2, 0), (1, 1), (3, 1), (2, 1)]
PLACE = {d: i for i, d in enumerate(ORDER)}


def slot(dx, dy, dc):
    return PLACE[(dx % NX, dy % 2)] * 2 + dc % 2


class Where:
    def __init__(self):
        self.e = lax.axis_index("expert")
        self.t = lax.axis_index("tok")
        self.c = lax.rem(self.t, 2)
        self.x = lax.rem(self.t // 2, NX)
        self.y = self.t // (2 * NX)

    def tok(self, dx, dy, dc):
        return (
            lax.rem(self.y + dy, 2) * NX + lax.rem(self.x + dx, NX)
        ) * 2 + lax.rem(self.c + dc, 2)

    def tok_dev(self, dx, dy, dc):
        return {"tok": self.tok(dx, dy, dc)}

    def exp(self, k):
        return lax.rem(self.e + k, NE)


NEAR = [(0, 0, 1), (0, 1, 0), (1, 0, 0), (3, 0, 0), (2, 0, 0)]


def greet(w, behind=False):
    barrier = pltpu.get_barrier_semaphore()
    for d in NEAR:
        pl.semaphore_signal(barrier, inc=1, device_id=w.tok_dev(*d), device_id_type=MESH)
    for k in range(1, NE):
        pl.semaphore_signal(barrier, inc=1, device_id={"expert": w.exp(k)}, device_id_type=MESH)
    if behind:
        back = lax.rem(w.t + 4 * NX - 1, 4 * NX)
        pl.semaphore_signal(barrier, inc=1, device_id={"tok": back}, device_id_type=MESH)
    pl.semaphore_wait(barrier, len(NEAR) + NE - 1 + behind)


class Mail:
    def __init__(self, sems):
        self.sems, self.out = sems, []

    def send(self, src, dst, rsem, dev):
        cp = pltpu.make_async_remote_copy(
            src_ref=src, dst_ref=dst, send_sem=self.sems.at[len(self.out)], recv_sem=rsem,
            device_id=dev, device_id_type=MESH,
        )
        cp.start()
        self.out.append(cp)

    def got(self, ref, rsem, dev):
        pltpu.make_async_remote_copy(
            src_ref=ref, dst_ref=ref, send_sem=self.sems.at[0], recv_sem=rsem,
            device_id=dev, device_id_type=MESH,
        ).wait_recv()

    def drain(self):
        for cp in self.out:
            cp.wait_send()


class Gather:
    def __init__(self, w, mail, view, rsems):
        self.w, self.mail, self.view, self.rsems = w, mail, view, rsems

    def put(self, frm, part, to, seen):
        s = slot(*seen)
        self.mail.send(
            self.view(slot(*frm), part), self.view(s, part), self.rsems.at[s, part],
            self.w.tok_dev(*to),
        )

    def got(self, dx, dy, dc, part):
        s = slot(dx, dy, dc)
        self.mail.got(self.view(s, part), self.rsems.at[s, part], self.w.tok_dev(0, 0, 1))

    def start(self, part):
        self.own_y(part)
        self.own_x(part)
        self.put((0, 0, 0), part, (0, 0, 1), (0, 0, 1))

    def own_y(self, part):
        self.put((0, 0, 0), part, (0, 1, 0), (0, 1, 0))

    def own_x(self, part):
        for dx in (1, 3, 2):
            self.put((0, 0, 0), part, (dx, 0, 0), (-dx, 0, 0))

    def sib(self, dx, dy, part):
        self.put((dx, dy, 0), part, (0, 0, 1), (dx, dy, 1))

    def y_in(self, part):
        self.got(0, 1, 0, part)
        if part == 1:
            for dx in (1, 3, 2):
                self.put((0, 1, 0), 1, (dx, 0, 0), (-dx, 1, 0))
        self.sib(0, 1, part)

    def x_in(self, dx):
        self.got(dx, 0, 0, 0)
        self.put((dx, 0, 0), 0, (0, 1, 0), (dx, 1, 0))
        self.sib(dx, 0, 0)

    def x_in_late(self, dx):
        self.got(dx, 0, 0, 1)
        self.sib(dx, 0, 1)

    def far_in(self, dx):
        for part in (0, 1):
            self.got(dx, 1, 0, part)
            self.sib(dx, 1, part)

    def sib_in(self, dx, dy):
        for part in (0, 1):
            self.got(dx, dy, 1, part)


AG_SENDS = 2 + 3 + 3 + 2 + (3 + 2) + 3 * 2 + 3 + 3 * 2


def rms(hid, gain):
    ms = jnp.mean(hid * hid, axis=-1, keepdims=True)
    return hid * lax.rsqrt(ms + 1e-05) * gain


def mixer_kernel(
    x_hbm, cw_hbm, b_hbm, c_hbm, ld_hbm, ds_hbm, wout_ref, gain_hbm,
    hid_ref, nrm_ref,
    x_ref, cw_ref, b_ref, c_ref, ld_ref, ds_ref, gain_ref,
    g_ref, part_ref, rec_ref, ext_ref, tail_ref, conv_ref, y_ref, ent_ref, st_ref, s1_ref, s2_ref,
    r_in_ref, r_out_ref, sin_ref, hand_ref, scan_ref,
    ssem, rsem, esem, tsem, usem, lsem,
):
    w = Where()
    mail = Mail(ssem)
    loads = [
        pltpu.make_async_copy(src, dst, lsem.at[i])
        for i, (src, dst) in enumerate((
            (x_hbm, x_ref), (wout_ref, g_ref.at[0]), (cw_hbm, cw_ref), (ld_hbm, ld_ref),
            (b_hbm, b_ref), (c_hbm, c_ref), (ds_hbm, ds_ref), (gain_hbm, gain_ref),
        ))
    ]
    for cp in loads:
        cp.start()
    toks, chans = x_ref.shape
    heads = ld_ref.shape[0]
    half = chans // 2
    n_state = b_ref.shape[1]
    depth, width = wout_ref.shape
    cut = depth * 5 // 8
    sib = w.tok_dev(0, 0, 1)
    greet(w, behind=True)
    loads[0].wait()
    mail.send(
        x_ref.at[pl.ds(toks - 16, 16)], tail_ref, tsem.at[0], {"tok": lax.rem(w.t + 1, 4 * NX)}
    )

    def view(s, part):
        return g_ref.at[s, pl.ds(0, cut)] if part == 0 else g_ref.at[s, pl.ds(cut, depth - cut)]

    ag = Gather(w, mail, view, rsem)
    loads[1].wait()
    ag.own_x(0)
    ag.own_y(0)
    ag.own_y(1)
    for cp in loads[2:]:
        cp.wait()

    ext_ref[16:, :] = x_ref[...].astype(f32)
    mail.got(tail_ref, tsem.at[0], sib)
    ext_ref[0:16, :] = jnp.where(w.t > 0, tail_ref[...].astype(f32), 0.0)
    for b in range(chans // 256):
        cols = pl.ds(b * 256, 256)
        v = cw_ref[0:1, cols] * ext_ref[13 : 13 + toks, cols]
        for k in range(1, CONV):
            v = v + cw_ref[k : k + 1, cols] * ext_ref[13 + k : 13 + k + toks, cols]
        conv_ref[:, cols] = v / (1.0 + jnp.exp(-v))

    ii = lax.broadcasted_iota(jnp.int32, (toks, toks), 0)
    jj = lax.broadcasted_iota(jnp.int32, (toks, toks), 1)
    low = ii >= jj
    lowf = jnp.where(low, 1.0, 0.0)
    cum = lax.dot_general(
        lowf, ld_ref[...], (((1,), (1,)), ((), ())),
        precision=highest, preferred_element_type=f32,
    )
    cum_t = jnp.dot(
        ld_ref[...], jnp.where(ii <= jj, 1.0, 0.0), precision=highest, preferred_element_type=f32
    )
    eh = lax.broadcasted_iota(jnp.int32, (heads, chans), 0) * HEAD
    ec = lax.broadcasted_iota(jnp.int32, (heads, chans), 1)
    spread = jnp.where((ec >= eh) & (ec < eh + HEAD), 1.0, 0.0)
    both = jnp.concatenate([cum, cum[toks - 1 : toks] - cum], axis=0)
    skip = jnp.dot(ds_ref[...], spread, precision=highest, preferred_element_type=f32)
    for h in range(2):
        for b in range(2):
            cols = pl.ds(h * half + b * (half // 2), half // 2)
            here = pl.ds(b * (half // 2), half // 2)
            sp = spread[:, h * half + b * (half // 2) : h * half + (b + 1) * (half // 2)]
            lev = jnp.exp(jnp.dot(both, sp, precision=highest, preferred_element_type=f32))
            ent_ref[:, cols] = lev[:toks]
            total = lev[toks - 1 : toks]
            xw = (conv_ref[:, cols] * lev[toks:]).astype(bf16)
            st_ref[h, 0:n_state, here] = lax.dot_general(
                b_ref[...], xw, (((0,), (0,)), ((), ())), preferred_element_type=f32
            ).astype(bf16)
            hi = total.astype(bf16).astype(f32)
            row = lax.broadcasted_iota(jnp.int32, (16, half // 2), 0)
            st_ref[h, n_state : n_state + 16, here] = jnp.where(row == 0, hi, total - hi).astype(bf16)

    mail.send(st_ref.at[1 - w.c], s1_ref, usem.at[0], sib)

    scores = lax.dot_general(
        c_ref[...], b_ref[...], (((1,), (1,)), ((), ())), preferred_element_type=f32
    )
    scores = jnp.where(low, scores, 0.0)
    lane = lax.broadcasted_iota(jnp.int32, (toks, 2 * HEAD), 1)

    def inside(p):
        cols = pl.ds(p * 2 * HEAD, 2 * HEAD)
        xc = conv_ref[:, cols]
        mats = []
        for h in (2 * p, 2 * p + 1):
            gap = jnp.where(low, cum[:, h : h + 1] - cum_t[h : h + 1, :], 0.0)
            mats.append((jnp.exp(gap) * scores).astype(bf16))
        yy = jnp.dot(jnp.concatenate(mats, axis=0), xc.astype(bf16), preferred_element_type=f32)
        y_ref[:, cols] = (
            jnp.where(lane < HEAD, yy[:toks], yy[toks:])
            + skip[:, p * 2 * HEAD : (p + 1) * 2 * HEAD] * xc
        )

    for p in range(2):
        inside(p)

    def by_rows(body):
        @pl.loop(0, n_state // 16)
        def _(i):
            body(pl.ds(pl.multiple_of(i * 16, 16), 16))

    def decay_of(block):
        v = block.astype(f32)
        return v[0:1] + v[1:2]

    DEC = pl.ds(n_state, 16)
    mail.got(s1_ref, usem.at[0], sib)
    own_d = decay_of(st_ref[w.c, DEC, :])
    sib_d = decay_of(s1_ref[DEC, :])
    first = w.c == 0
    d0 = jnp.where(first, own_d, sib_d)
    d1 = jnp.where(first, sib_d, own_d)
    chip_d = d0 * d1
    chip_hi = chip_d.astype(bf16).astype(f32)
    row = lax.broadcasted_iota(jnp.int32, (16, half), 0)
    s2_ref[w.x, DEC, :] = jnp.where(row == 0, chip_hi, chip_d - chip_hi).astype(bf16)

    def join(r):
        own, other = st_ref[w.c, r, :].astype(f32), s1_ref[r, :].astype(f32)
        s2_ref[w.x, r, :] = (
            d1 * jnp.where(first, own, other) + jnp.where(first, other, own)
        ).astype(bf16)

    by_rows(join)
    for i, dx in enumerate((1, 3, 2)):
        mail.send(s2_ref.at[w.x], s2_ref.at[w.x], tsem.at[1 + NX - dx], w.tok_dev(dx, 0, 0))
    ag.own_x(1)
    for part in (0, 1):
        ag.put((0, 0, 0), part, (0, 0, 1), (0, 0, 1))
    for p in range(2, heads // 2):
        inside(p)
    ag.y_in(0)
    ag.y_in(1)
    ag.x_in(1)
    for dx in (1, 3, 2):
        mail.got(s2_ref.at[lax.rem(w.x + dx, NX)], tsem.at[1 + dx], w.tok_dev(dx, 0, 0))
    decs = [decay_of(s2_ref[k, DEC, :]) for k in range(NX)]
    before_d = jnp.ones_like(chip_d)
    for k in range(NX):
        before_d = before_d * jnp.where(w.x > k, decs[k], 1.0)

    def row_scan(r):
        run = jnp.zeros((16, half), f32)
        before = run
        for k in range(NX):
            before = jnp.where(w.x == k, run, before)
            run = decs[k] * run + s2_ref[k, r, :].astype(f32)
        r_out_ref[0, r, :] = run.astype(bf16)
        r_out_ref[1, r, :] = before.astype(bf16)

    by_rows(row_scan)
    mail.send(r_out_ref.at[0], r_in_ref, usem.at[1], w.tok_dev(0, 1, 0))
    ag.x_in(3)
    ag.x_in(2)
    mail.got(r_in_ref, usem.at[1], w.tok_dev(0, 1, 0))
    lower = w.y > 0

    def enter(r):
        chip = r_out_ref[1, r, :].astype(f32) + jnp.where(
            lower, before_d * r_in_ref[r, :].astype(f32), 0.0
        )
        s0 = jnp.where(first, st_ref[w.c, r, :], s1_ref[r, :]).astype(f32)
        second = d0 * chip + s0
        sin_ref[w.c, r, :] = jnp.where(first, chip, second).astype(bf16)
        hand_ref[r, :] = jnp.where(first, second, chip).astype(bf16)

    by_rows(enter)
    mail.send(hand_ref, sin_ref.at[w.c], usem.at[2], sib)

    def close(h):
        for b in range(2):
            cols = pl.ds(pl.multiple_of(h * half + b * (half // 2), half // 2), half // 2)
            here = pl.ds(b * (half // 2), half // 2)
            carry = jnp.dot(c_ref[...], sin_ref[h, :, here], preferred_element_type=f32)
            scan_ref[:, cols] = (y_ref[:, cols] + ent_ref[:, cols] * carry).astype(bf16)

    close(w.c)
    mail.got(sin_ref.at[1 - w.c], usem.at[2], sib)
    close(1 - w.c)

    def mult(dx, dy, dc):
        cols = pl.ds(pl.multiple_of(w.tok(dx, dy, dc) * width, width), width)
        part_ref[:, cols] = jnp.dot(
            scan_ref[...], g_ref[slot(dx, dy, dc)], preferred_element_type=f32
        ).astype(bf16)

    rows = hid_ref.shape[0]

    def mine(e):
        return pl.ds(pl.multiple_of(e * rows, rows), rows)

    def out(dx, dy):
        chip = (w.tok(dx, dy, 0) // 2) * 2 * width
        cols = pl.ds(pl.multiple_of(chip, 2 * width), 2 * width)
        for k in range(1, NE):
            mail.send(
                part_ref.at[mine(w.exp(k)), cols], rec_ref.at[k - 1, :, cols], esem.at[k - 1],
                {"expert": w.exp(k)},
            )

    def pair(dx, dy):
        mult(dx, dy, 0)
        ag.sib_in(dx, dy)
        mult(dx, dy, 1)
        out(dx, dy)

    for dx in (1, 3, 2):
        ag.x_in_late(dx)
    for d in ((0, 0), (0, 1), (1, 0), (3, 0), (2, 0)):
        pair(*d)
    for dx in (1, 3, 2):
        ag.far_in(dx)
    for dx in (1, 3, 2):
        pair(dx, 1)
    total = part_ref[mine(w.e), :].astype(f32)
    for k in range(1, NE):
        mail.got(rec_ref.at[k - 1], esem.at[k - 1], {"expert": w.exp(k)})
        total = total + rec_ref[k - 1].astype(f32)
    hid_b = total.astype(bf16)
    hid_ref[...] = hid_b
    nrm_ref[...] = rms(hid_b.astype(f32), gain_ref[...]).astype(bf16)
    mail.drain()


def mixer(x_in, conv_w, b_proj, c_proj, log_decay, d_skip, w_out, gain, rows):
    depth, width = w_out.shape
    toks, chans = x_in.shape
    model, n_state = gain.shape[1], b_proj.shape[1]
    half = chans // 2
    small = (x_in, conv_w, b_proj, c_proj, log_decay, d_skip, gain)
    vm = pl.BlockSpec(memory_space=pltpu.VMEM)
    dma = pltpu.SemaphoreType.DMA
    return pl.pallas_call(
        mixer_kernel,
        out_shape=[jax.ShapeDtypeStruct((rows, model), bf16)] * 2,
        in_specs=[pl.BlockSpec(memory_space=pl.ANY)] * 8,
        out_specs=[vm] * 2,
        scratch_shapes=[
            *[pltpu.VMEM(a.shape, a.dtype) for a in small],
            pltpu.VMEM((16, depth, width), bf16),
            pltpu.VMEM((toks, model), bf16),
            pltpu.VMEM((NE - 1, rows, model), bf16),
            pltpu.VMEM((toks + 16, chans), f32),
            pltpu.VMEM((16, chans), bf16),
            pltpu.VMEM((toks, chans), f32),
            pltpu.VMEM((toks, chans), f32),
            pltpu.VMEM((toks, chans), f32),
            pltpu.VMEM((2, n_state + 16, half), bf16),
            pltpu.VMEM((n_state + 16, half), bf16),
            pltpu.VMEM((NX, n_state + 16, half), bf16),
            pltpu.VMEM((n_state, half), bf16),
            pltpu.VMEM((2, n_state, half), bf16),
            pltpu.VMEM((2, n_state, half), bf16),
            pltpu.VMEM((n_state, half), bf16),
            pltpu.VMEM((toks, chans), bf16),
            dma((AG_SENDS + 8 * (NE - 1) + 7,)),
            dma((16, 2)),
            dma((NE - 1,)),
            dma((1 + NX,)),
            dma((3,)),
            dma((8,)),
        ],
        compiler_params=pltpu.CompilerParams(
            collective_id=1, has_side_effects=True, vmem_limit_bytes=56 * 2**20
        ),
        cost_estimate=pl.CostEstimate(
            flops=2 * toks * depth * model, bytes_accessed=20 * 2**20, transcendentals=0
        ),
        name="mixer",
    )(x_in, conv_w, b_proj, c_proj, log_decay, d_skip, w_out, gain)


def expert_kernel(
    nrm_ref, rt_ref, hid_ref, wr_ref, we_ref, out_ref,
    wv_ref, n_ref, r_ref, g_ref, a_ref, o_ref, sib_ref, yp_ref, yq_ref, xp_ref, xq_ref,
    con_ref, rec_ref, own_ref,
    lsem, ssem, nsem, tsem, gsem, bsem, psem, qsem, fsem, esem,
):
    w = Where()
    mail = Mail(ssem)
    rows, model = nrm_ref.shape
    cap = g_ref.shape[1]
    hidden = wv_ref.shape[2]
    toks = n_ref.shape[0]
    cut = model * 5 // 8
    P, Q = pl.ds(0, cut), pl.ds(cut, model - cut)
    loads = [pltpu.make_async_copy(we_ref.at[0, i], wv_ref.at[i], lsem.at[i]) for i in range(3)]
    for cp in loads:
        cp.start()
    lane = lax.broadcasted_iota(jnp.int32, (rows, 128), 1)
    ids = rt_ref[...].astype(f32)
    own_ref[...] = jnp.where(lane == 0, ids[:, 0:1], ids[:, 1:2]).astype(bf16)
    greet(w)

    def of(e):
        return pl.ds(pl.multiple_of(e * rows, rows), rows)

    me = of(w.e)
    for k in range(1, NE):
        mail.send(own_ref, r_ref.at[me], tsem.at[k - 1], {"expert": w.exp(k)})
    for i, cols in enumerate((P, Q)):
        for k in range(1, NE):
            mail.send(
                nrm_ref.at[:, cols], n_ref.at[me, cols], nsem.at[i, k - 1], {"expert": w.exp(k)}
            )
    n_ref[me, :] = nrm_ref[...]
    r_ref[me, :] = own_ref[...]
    for k in range(1, NE):
        mail.got(r_ref.at[of(w.exp(NE - k))], tsem.at[k - 1], {"expert": w.exp(k)})

    ii = lax.broadcasted_iota(jnp.int32, (toks, toks), 0)
    jj = lax.broadcasted_iota(jnp.int32, (toks, toks), 1)
    eye = (ii == jj).astype(f32)
    r1 = r_ref[:, 0:1].astype(f32)
    r2 = r_ref[:, 1:2].astype(f32)
    e_f = w.e.astype(f32)
    hit = jnp.where(r1 == e_f, 1.0, 0.0) + jnp.where(r2 == e_f, 1.0, 0.0)
    rank = jnp.sum(jnp.where(ii < jj, hit, 0.0), axis=0, keepdims=True)
    hit_row = jnp.sum(hit * eye, axis=0, keepdims=True)
    want = lax.broadcasted_iota(jnp.int32, (cap, toks), 0).astype(f32)
    sel_f = jnp.where(want == rank, 1.0, 0.0) * hit_row
    sel = sel_f.astype(bf16)

    def view(s, part):
        return g_ref.at[s, :, Q if part else P]

    ag = Gather(w, mail, view, gsem)
    for i, cols in enumerate((P, Q)):
        for k in range(1, NE):
            mail.got(n_ref.at[of(w.exp(NE - k)), cols], nsem.at[i, k - 1], {"expert": w.exp(k)})
        g_ref[0, :, cols] = jnp.dot(sel, n_ref[:, cols], preferred_element_type=f32).astype(bf16)
        ag.start(i)

    logits = lax.dot_general(
        n_ref[...], wr_ref[...], (((1,), (1,)), ((), ())), preferred_element_type=f32
    )
    lane = lax.broadcasted_iota(jnp.int32, logits.shape, 1).astype(f32)
    s1 = jax.nn.sigmoid(jnp.sum(jnp.where(lane == r1, logits, 0.0), axis=1, keepdims=True))
    s2 = jax.nn.sigmoid(jnp.sum(jnp.where(lane == r2, logits, 0.0), axis=1, keepdims=True))
    gate = jnp.where(r1 == e_f, s1, s2) / (s1 + s2)
    gate_row = jnp.sum(gate * eye, axis=0, keepdims=True)
    gate_col = jnp.sum(sel_f * gate_row, axis=1, keepdims=True)

    def compute(group):
        xs = pl.ds(group * 4, 4)
        tile = 1024
        xg = g_ref[xs].reshape(4 * cap, model)
        gv = jnp.dot(xg, wv_ref[0], preferred_element_type=f32)
        uv = jnp.dot(xg, wv_ref[1], preferred_element_type=f32)
        a_ref[...] = (gv / (1.0 + jnp.exp(-gv)) * uv).astype(bf16)
        if group == 0:
            loads[2].wait()

        @pl.loop(0, model // tile)
        def _(i):
            cols = pl.ds(pl.multiple_of(i * tile, tile), tile)
            o = lax.dot_general(
                a_ref[...], wv_ref[2, cols, :], (((1,), (1,)), ((), ())), preferred_element_type=f32
            )
            o_ref[xs, :, cols] = o.astype(bf16).reshape(4, cap, tile)

    def add(dst, cols, *srcs):
        @pl.loop(0, cap // 16)
        def _(i):
            r = pl.ds(pl.multiple_of(i * 16, 16), 16)
            v = o_ref[dst, r, cols].astype(f32)
            for src in srcs:
                v = v + src(r).astype(f32)
            o_ref[dst, r, cols] = v.astype(bf16)

    def pair_out(group):
        for p in (0, 1):
            i = group * 2 + p
            mail.send(o_ref.at[i * 2 + 1], sib_ref.at[i], bsem.at[i], w.tok_dev(0, 0, 1))

    def pair_in(group):
        for p in (0, 1):
            i = group * 2 + p
            dx, dy = ORDER[i]
            mail.got(sib_ref.at[i], bsem.at[i], w.tok_dev(0, 0, 1))
            add(i * 2, slice(None), lambda r, i=i: sib_ref[i, r, :])
            if dy == 1:
                mail.send(o_ref.at[i * 2, :, P], yp_ref.at[dx], psem.at[dx], w.tok_dev(0, 1, 0))
            if dx != 0:
                b = (NX - dx - 1) * 2 + dy
                mail.send(o_ref.at[i * 2, :, Q], xq_ref.at[b], qsem.at[b], w.tok_dev(dx, 0, 0))

    def y_sum(dx):
        mail.got(yp_ref.at[dx], psem.at[dx], w.tok_dev(0, 1, 0))
        add(slot(dx, 0, 0), P, lambda r: yp_ref[dx, r, :])
        if dx != 0:
            b = NX - dx - 1
            mail.send(o_ref.at[slot(dx, 0, 0), :, P], xp_ref.at[b], fsem.at[b], w.tok_dev(dx, 0, 0))

    def x_sum(dy):
        for b in range(3):
            mail.got(xq_ref.at[b * 2 + dy], qsem.at[b * 2 + dy], w.tok_dev(1, 0, 0))
        add(slot(0, dy, 0), Q, *[lambda r, b=b: xq_ref[b * 2 + dy, r, :] for b in range(3)])
        if dy == 1:
            mail.send(o_ref.at[slot(0, 1, 0), :, Q], yq_ref, fsem.at[3], w.tok_dev(0, 1, 0))

    ag.y_in(0)
    ag.x_in(1)
    ag.x_in(3)
    ag.y_in(1)
    ag.x_in(2)
    ag.sib_in(0, 0)
    ag.sib_in(0, 1)
    loads[0].wait()
    loads[1].wait()
    compute(0)
    pair_out(0)
    for dx in (1, 3, 2):
        ag.x_in_late(dx)
    ag.sib_in(1, 0)
    ag.sib_in(3, 0)
    compute(1)
    pair_out(1)
    pair_in(0)
    ag.far_in(1)
    ag.sib_in(2, 0)
    ag.sib_in(1, 1)
    compute(2)
    pair_out(2)
    ag.far_in(3)
    ag.far_in(2)
    pair_in(1)
    ag.sib_in(3, 1)
    ag.sib_in(2, 1)
    compute(3)
    pair_out(3)
    pair_in(2)
    y_sum(1)
    pair_in(3)
    x_sum(1)
    y_sum(3)
    y_sum(2)
    y_sum(0)
    x_sum(0)

    def final(i, cols, srcs):
        v = o_ref[0, :, cols].astype(f32)
        for src in srcs:
            v = v + src.astype(f32)
        con_ref[:, cols] = lax.dot_general(
            sel, (v * gate_col).astype(bf16), (((0,), (0,)), ((), ())), preferred_element_type=f32
        ).astype(bf16)
        for k in range(1, NE):
            mail.send(
                con_ref.at[of(w.exp(k)), cols], rec_ref.at[k - 1, :, cols], esem.at[i, k - 1],
                {"expert": w.exp(k)},
            )

    def finish(i, cols):
        total = hid_ref[:, cols].astype(f32) + con_ref[me, cols].astype(f32)
        for k in range(1, NE):
            mail.got(rec_ref.at[k - 1, :, cols], esem.at[i, k - 1], {"expert": w.exp(k)})
            total = total + rec_ref[k - 1, :, cols].astype(f32)
        out_ref[:, cols] = total.astype(bf16)

    mail.got(yq_ref, fsem.at[3], w.tok_dev(0, 1, 0))
    final(1, Q, [yq_ref[...]])
    for b in range(3):
        mail.got(xp_ref.at[b], fsem.at[b], w.tok_dev(1, 0, 0))
    final(0, P, [xp_ref[b] for b in range(3)])
    finish(1, Q)
    finish(0, P)
    mail.drain()


def expert_layer(normed, route, hidden, w_router, w_expert):
    rows, model = normed.shape
    units = w_expert.shape[3]
    toks, cap = rows * NE, 80
    cut = model * 5 // 8
    vm = pl.BlockSpec(memory_space=pltpu.VMEM)
    sends = 5 * (NE - 1) + AG_SENDS + 8 + 4 + 6 + 3 + 1
    dma = pltpu.SemaphoreType.DMA
    return pl.pallas_call(
        expert_kernel,
        out_shape=jax.ShapeDtypeStruct((rows, model), bf16),
        in_specs=[vm] * 4 + [pl.BlockSpec(memory_space=pl.ANY)],
        out_specs=vm,
        scratch_shapes=[
            pltpu.VMEM((3, model, units), bf16),
            pltpu.VMEM((toks, model), bf16),
            pltpu.VMEM((toks, 128), bf16),
            pltpu.VMEM((16, cap, model), bf16),
            pltpu.VMEM((4 * cap, units), bf16),
            pltpu.VMEM((16, cap, model), bf16),
            pltpu.VMEM((8, cap, model), bf16),
            pltpu.VMEM((4, cap, cut), bf16),
            pltpu.VMEM((cap, model - cut), bf16),
            pltpu.VMEM((3, cap, cut), bf16),
            pltpu.VMEM((6, cap, model - cut), bf16),
            pltpu.VMEM((toks, model), bf16),
            pltpu.VMEM((NE - 1, rows, model), bf16),
            pltpu.VMEM((rows, 128), bf16),
            dma((3,)), dma((sends,)), dma((2, NE - 1)), dma((NE - 1,)), dma((16, 2)), dma((8,)),
            dma((4,)), dma((6,)), dma((4,)), dma((2, NE - 1)),
        ],
        compiler_params=pltpu.CompilerParams(
            collective_id=2, has_side_effects=True, vmem_limit_bytes=60 * 2**20
        ),
        cost_estimate=pl.CostEstimate(
            flops=6 * 16 * cap * model * units, bytes_accessed=20 * 2**20, transcendentals=0
        ),
        name="expert_layer",
    )(normed, route, hidden, w_router, w_expert)


def on_device(
    x_in, conv_w, b_proj, c_proj, log_decay, d_skip, w_out, norm_gain, w_router, w_expert, route_ids
):
    rows, model = route_ids.shape[1], norm_gain.shape[0]
    hidden, normed = mixer(
        x_in, conv_w, b_proj, c_proj, log_decay.T, d_skip[None], w_out, norm_gain[None], rows
    )
    layer_out = expert_layer(normed, route_ids[0], hidden, w_router.T, w_expert)
    return layer_out.reshape(1, rows, model)


def solution(mesh):
    placed = (
        P("tok", "expert"),
        P(None, "expert"),
        P("tok", None),
        P("tok", None),
        P("tok", "expert"),
        P("expert"),
        P("expert", "tok"),
        P(),
        P(),
        P("expert", None, None, "tok"),
        P("tok", "expert", None),
    )
    return jax.shard_map(
        on_device, mesh=mesh, in_specs=placed, out_specs=P("tok", "expert", None), check_vma=False
    )
```

```python
import jax
import jax.numpy as jnp
from jax import lax
from jax.experimental import pallas as pl
from jax.experimental.pallas import tpu as pltpu
from jax.sharding import PartitionSpec as P

CONV = 4
HEAD = 64
highest = lax.Precision.HIGHEST
MESH = pl.DeviceIdType.MESH
bf16, f32 = jnp.bfloat16, jnp.float32
NX, NE = 4, 8
ORDER = [(0, 0), (0, 1), (1, 0), (3, 0), (2, 0), (1, 1), (3, 1), (2, 1)]
PLACE = {d: i for i, d in enumerate(ORDER)}


def slot(dx, dy, dc):
    return PLACE[(dx % NX, dy % 2)] * 2 + dc % 2


class Where:
    def __init__(self):
        self.e = lax.axis_index("expert")
        self.t = lax.axis_index("tok")
        self.c = lax.rem(self.t, 2)
        self.x = lax.rem(self.t // 2, NX)
        self.y = self.t // (2 * NX)

    def tok(self, dx, dy, dc):
        return (
            lax.rem(self.y + dy, 2) * NX + lax.rem(self.x + dx, NX)
        ) * 2 + lax.rem(self.c + dc, 2)

    def tok_dev(self, dx, dy, dc):
        return {"tok": self.tok(dx, dy, dc)}

    def exp(self, k):
        return lax.rem(self.e + k, NE)


NEAR = [(0, 0, 1), (0, 1, 0), (1, 0, 0), (3, 0, 0), (2, 0, 0)]


def greet(w, behind=False):
    barrier = pltpu.get_barrier_semaphore()
    for d in NEAR:
        pl.semaphore_signal(barrier, inc=1, device_id=w.tok_dev(*d), device_id_type=MESH)
    for k in range(1, NE):
        pl.semaphore_signal(barrier, inc=1, device_id={"expert": w.exp(k)}, device_id_type=MESH)
    if behind:
        back = lax.rem(w.t + 4 * NX - 1, 4 * NX)
        pl.semaphore_signal(barrier, inc=1, device_id={"tok": back}, device_id_type=MESH)
    pl.semaphore_wait(barrier, len(NEAR) + NE - 1 + behind)


class Mail:
    def __init__(self, sems):
        self.sems, self.out = sems, []

    def send(self, src, dst, rsem, dev):
        cp = pltpu.make_async_remote_copy(
            src_ref=src, dst_ref=dst, send_sem=self.sems.at[len(self.out)], recv_sem=rsem,
            device_id=dev, device_id_type=MESH,
        )
        cp.start()
        self.out.append(cp)

    def got(self, ref, rsem, dev):
        pltpu.make_async_remote_copy(
            src_ref=ref, dst_ref=ref, send_sem=self.sems.at[0], recv_sem=rsem,
            device_id=dev, device_id_type=MESH,
        ).wait_recv()

    def drain(self):
        for cp in self.out:
            cp.wait_send()


class Gather:
    def __init__(self, w, mail, view, rsems):
        self.w, self.mail, self.view, self.rsems = w, mail, view, rsems

    def put(self, frm, part, to, seen):
        s = slot(*seen)
        self.mail.send(
            self.view(slot(*frm), part), self.view(s, part), self.rsems.at[s, part],
            self.w.tok_dev(*to),
        )

    def got(self, dx, dy, dc, part):
        s = slot(dx, dy, dc)
        self.mail.got(self.view(s, part), self.rsems.at[s, part], self.w.tok_dev(0, 0, 1))

    def own_y(self, part):
        self.put((0, 0, 0), part, (0, 1, 0), (0, 1, 0))

    def own_sib(self, part):
        self.put((0, 0, 0), part, (0, 0, 1), (0, 0, 1))

    def along_x(self, dy, part):
        for dx in (1, 3):
            self.put((0, dy, 0), part, (dx, 0, 0), (-dx, dy, 0))

    def own(self, part):
        self.own_y(part)
        self.along_x(0, part)
        self.own_sib(part)

    def arrive(self, dx, dy, part):
        self.got(dx, dy, 0, part)
        on = (3, 1, 3, 1)[part]
        if dx == (NX - on) and (part > 1 or dy == 0):
            self.put((dx, dy, 0), part, (on, 0, 0), (2, dy, 0))
        if part < 2 and dx != 0 and dy == 0:
            self.put((dx, 0, 0), part, (0, 1, 0), (dx, 1, 0))
        if part > 1 and dx == 0:
            self.along_x(1, part)
        self.put((dx, dy, 0), part, (0, 0, 1), (dx, dy, 1))

    def sib_in(self, dx, dy):
        for part in range(4):
            self.got(dx, dy, 1, part)


AG_SENDS = 60


def rms(hid, gain):
    ms = jnp.mean(hid * hid, axis=-1, keepdims=True)
    return hid * lax.rsqrt(ms + 1e-05) * gain


def mixer_kernel(
    x_hbm, cw_hbm, b_hbm, c_hbm, ld_hbm, ds_hbm, wout_ref, gain_hbm,
    hid_ref, nrm_ref,
    x_ref, cw_ref, b_ref, c_ref, ld_ref, ds_ref, gain_ref,
    g_ref, part_ref, rec_ref, ext_ref, tail_ref, conv_ref, y_ref, ent_ref, st_ref, s1_ref, s2_ref,
    r_in_ref, r_out_ref, sin_ref, hand_ref, scan_ref,
    ssem, rsem, esem, tsem, usem, lsem,
):
    w = Where()
    mail = Mail(ssem)
    loads = [
        pltpu.make_async_copy(src, dst, lsem.at[i])
        for i, (src, dst) in enumerate((
            (x_hbm, x_ref), (wout_ref, g_ref.at[0]), (cw_hbm, cw_ref), (ld_hbm, ld_ref),
            (b_hbm, b_ref), (c_hbm, c_ref), (ds_hbm, ds_ref), (gain_hbm, gain_ref),
        ))
    ]
    for cp in loads:
        cp.start()
    toks, chans = x_ref.shape
    heads = ld_ref.shape[0]
    half = chans // 2
    n_state = b_ref.shape[1]
    depth, width = wout_ref.shape
    cut = depth // 4
    sib = w.tok_dev(0, 0, 1)
    greet(w, behind=True)
    loads[0].wait()
    mail.send(
        x_ref.at[pl.ds(toks - 16, 16)], tail_ref, tsem.at[0], {"tok": lax.rem(w.t + 1, 4 * NX)}
    )

    def view(s, part):
        return g_ref.at[s, pl.ds(part * cut, cut)]

    ag = Gather(w, mail, view, rsem)
    loads[1].wait()
    for part in (0, 1):
        ag.along_x(0, part)
    for part in (2, 0, 3, 1):
        ag.own_y(part)
    for cp in loads[2:]:
        cp.wait()

    ext_ref[16:, :] = x_ref[...].astype(f32)
    mail.got(tail_ref, tsem.at[0], sib)
    ext_ref[0:16, :] = jnp.where(w.t > 0, tail_ref[...].astype(f32), 0.0)
    for b in range(chans // 256):
        cols = pl.ds(b * 256, 256)
        v = cw_ref[0:1, cols] * ext_ref[13 : 13 + toks, cols]
        for k in range(1, CONV):
            v = v + cw_ref[k : k + 1, cols] * ext_ref[13 + k : 13 + k + toks, cols]
        conv_ref[:, cols] = v / (1.0 + jnp.exp(-v))

    ii = lax.broadcasted_iota(jnp.int32, (toks, toks), 0)
    jj = lax.broadcasted_iota(jnp.int32, (toks, toks), 1)
    low = ii >= jj
    lowf = jnp.where(low, 1.0, 0.0)
    cum = lax.dot_general(
        lowf, ld_ref[...], (((1,), (1,)), ((), ())),
        precision=highest, preferred_element_type=f32,
    )
    cum_t = jnp.dot(
        ld_ref[...], jnp.where(ii <= jj, 1.0, 0.0), precision=highest, preferred_element_type=f32
    )
    eh = lax.broadcasted_iota(jnp.int32, (heads, chans), 0) * HEAD
    ec = lax.broadcasted_iota(jnp.int32, (heads, chans), 1)
    spread = jnp.where((ec >= eh) & (ec < eh + HEAD), 1.0, 0.0)
    both = jnp.concatenate([cum, cum[toks - 1 : toks] - cum], axis=0)
    skip = jnp.dot(ds_ref[...], spread, precision=highest, preferred_element_type=f32)
    for h in range(2):
        for b in range(2):
            cols = pl.ds(h * half + b * (half // 2), half // 2)
            here = pl.ds(b * (half // 2), half // 2)
            sp = spread[:, h * half + b * (half // 2) : h * half + (b + 1) * (half // 2)]
            lev = jnp.exp(jnp.dot(both, sp, precision=highest, preferred_element_type=f32))
            ent_ref[:, cols] = lev[:toks]
            total = lev[toks - 1 : toks]
            xw = (conv_ref[:, cols] * lev[toks:]).astype(bf16)
            st_ref[h, 0:n_state, here] = lax.dot_general(
                b_ref[...], xw, (((0,), (0,)), ((), ())), preferred_element_type=f32
            ).astype(bf16)
            hi = total.astype(bf16).astype(f32)
            row = lax.broadcasted_iota(jnp.int32, (16, half // 2), 0)
            st_ref[h, n_state : n_state + 16, here] = jnp.where(row == 0, hi, total - hi).astype(bf16)

    mail.send(st_ref.at[1 - w.c], s1_ref, usem.at[0], sib)

    scores = lax.dot_general(
        c_ref[...], b_ref[...], (((1,), (1,)), ((), ())), preferred_element_type=f32
    )
    scores = jnp.where(low, scores, 0.0)
    lane = lax.broadcasted_iota(jnp.int32, (toks, 2 * HEAD), 1)

    def inside(p):
        cols = pl.ds(p * 2 * HEAD, 2 * HEAD)
        xc = conv_ref[:, cols]
        mats = []
        for h in (2 * p, 2 * p + 1):
            gap = jnp.where(low, cum[:, h : h + 1] - cum_t[h : h + 1, :], 0.0)
            mats.append((jnp.exp(gap) * scores).astype(bf16))
        yy = jnp.dot(jnp.concatenate(mats, axis=0), xc.astype(bf16), preferred_element_type=f32)
        y_ref[:, cols] = (
            jnp.where(lane < HEAD, yy[:toks], yy[toks:])
            + skip[:, p * 2 * HEAD : (p + 1) * 2 * HEAD] * xc
        )

    for p in range(2):
        inside(p)

    def by_rows(body):
        @pl.loop(0, n_state // 16)
        def _(i):
            body(pl.ds(pl.multiple_of(i * 16, 16), 16))

    def decay_of(block):
        v = block.astype(f32)
        return v[0:1] + v[1:2]

    DEC = pl.ds(n_state, 16)
    mail.got(s1_ref, usem.at[0], sib)
    own_d = decay_of(st_ref[w.c, DEC, :])
    sib_d = decay_of(s1_ref[DEC, :])
    first = w.c == 0
    d0 = jnp.where(first, own_d, sib_d)
    d1 = jnp.where(first, sib_d, own_d)
    chip_d = d0 * d1
    chip_hi = chip_d.astype(bf16).astype(f32)
    row = lax.broadcasted_iota(jnp.int32, (16, half), 0)
    s2_ref[w.x, DEC, :] = jnp.where(row == 0, chip_hi, chip_d - chip_hi).astype(bf16)

    def join(r):
        own, other = st_ref[w.c, r, :].astype(f32), s1_ref[r, :].astype(f32)
        s2_ref[w.x, r, :] = (
            d1 * jnp.where(first, own, other) + jnp.where(first, other, own)
        ).astype(bf16)

    by_rows(join)
    for i, dx in enumerate((1, 3, 2)):
        mail.send(s2_ref.at[w.x], s2_ref.at[w.x], tsem.at[1 + NX - dx], w.tok_dev(dx, 0, 0))
    for part in (2, 3):
        ag.along_x(0, part)
    for part in range(4):
        ag.own_sib(part)
    for p in range(2, heads // 2):
        inside(p)
    for d in ((1, 0, 0), (3, 0, 0), (0, 1, 2)):
        ag.arrive(*d)
    for dx in (1, 3, 2):
        mail.got(s2_ref.at[lax.rem(w.x + dx, NX)], tsem.at[1 + dx], w.tok_dev(dx, 0, 0))
    decs = [decay_of(s2_ref[k, DEC, :]) for k in range(NX)]
    before_d = jnp.ones_like(chip_d)
    for k in range(NX):
        before_d = before_d * jnp.where(w.x > k, decs[k], 1.0)

    def row_scan(r):
        run = jnp.zeros((16, half), f32)
        before = run
        for k in range(NX):
            before = jnp.where(w.x == k, run, before)
            run = decs[k] * run + s2_ref[k, r, :].astype(f32)
        r_out_ref[0, r, :] = run.astype(bf16)
        r_out_ref[1, r, :] = before.astype(bf16)

    by_rows(row_scan)
    mail.send(r_out_ref.at[0], r_in_ref, usem.at[1], w.tok_dev(0, 1, 0))
    for d in ((1, 0, 1), (3, 0, 1), (0, 1, 3), (0, 1, 0), (0, 1, 1), (2, 0, 0), (2, 0, 1)):
        ag.arrive(*d)
    mail.got(r_in_ref, usem.at[1], w.tok_dev(0, 1, 0))
    lower = w.y > 0

    def enter(r):
        chip = r_out_ref[1, r, :].astype(f32) + jnp.where(
            lower, before_d * r_in_ref[r, :].astype(f32), 0.0
        )
        s0 = jnp.where(first, st_ref[w.c, r, :], s1_ref[r, :]).astype(f32)
        second = d0 * chip + s0
        sin_ref[w.c, r, :] = jnp.where(first, chip, second).astype(bf16)
        hand_ref[r, :] = jnp.where(first, second, chip).astype(bf16)

    by_rows(enter)
    mail.send(hand_ref, sin_ref.at[w.c], usem.at[2], sib)

    for part in (2, 3):
        for d in ((1, 0, part), (3, 0, part)):
            ag.arrive(*d)

    def close(h):
        for b in range(2):
            cols = pl.ds(pl.multiple_of(h * half + b * (half // 2), half // 2), half // 2)
            here = pl.ds(b * (half // 2), half // 2)
            carry = jnp.dot(c_ref[...], sin_ref[h, :, here], preferred_element_type=f32)
            scan_ref[:, cols] = (y_ref[:, cols] + ent_ref[:, cols] * carry).astype(bf16)

    close(w.c)
    mail.got(sin_ref.at[1 - w.c], usem.at[2], sib)
    close(1 - w.c)

    def mult(dx, dy, dc):
        cols = pl.ds(pl.multiple_of(w.tok(dx, dy, dc) * width, width), width)
        part_ref[:, cols] = jnp.dot(
            scan_ref[...], g_ref[slot(dx, dy, dc)], preferred_element_type=f32
        ).astype(bf16)

    rows = hid_ref.shape[0]

    def mine(e):
        return pl.ds(pl.multiple_of(e * rows, rows), rows)

    def out(dx, dy):
        chip = (w.tok(dx, dy, 0) // 2) * 2 * width
        cols = pl.ds(pl.multiple_of(chip, 2 * width), 2 * width)
        for k in range(1, NE):
            mail.send(
                part_ref.at[mine(w.exp(k)), cols], rec_ref.at[k - 1, :, cols], esem.at[k - 1],
                {"expert": w.exp(k)},
            )

    def pair(dx, dy):
        mult(dx, dy, 0)
        ag.sib_in(dx, dy)
        mult(dx, dy, 1)
        out(dx, dy)

    for part in (2, 3):
        for d in ((1, 1, part), (3, 1, part), (2, 0, part)):
            ag.arrive(*d)
    for d in ((0, 0), (0, 1), (1, 0), (3, 0), (2, 0)):
        pair(*d)
    for dx in (1, 3):
        for part in (0, 1):
            ag.arrive(dx, 1, part)
        pair(dx, 1)
    for part in (2, 3, 0, 1):
        ag.arrive(2, 1, part)
    pair(2, 1)
    total = part_ref[mine(w.e), :].astype(f32)
    for k in range(1, NE):
        mail.got(rec_ref.at[k - 1], esem.at[k - 1], {"expert": w.exp(k)})
        total = total + rec_ref[k - 1].astype(f32)
    hid_b = total.astype(bf16)
    hid_ref[...] = hid_b
    nrm_ref[...] = rms(hid_b.astype(f32), gain_ref[...]).astype(bf16)
    mail.drain()


def mixer(x_in, conv_w, b_proj, c_proj, log_decay, d_skip, w_out, gain, rows):
    depth, width = w_out.shape
    toks, chans = x_in.shape
    model, n_state = gain.shape[1], b_proj.shape[1]
    half = chans // 2
    small = (x_in, conv_w, b_proj, c_proj, log_decay, d_skip, gain)
    vm = pl.BlockSpec(memory_space=pltpu.VMEM)
    dma = pltpu.SemaphoreType.DMA
    return pl.pallas_call(
        mixer_kernel,
        out_shape=[jax.ShapeDtypeStruct((rows, model), bf16)] * 2,
        in_specs=[pl.BlockSpec(memory_space=pl.ANY)] * 8,
        out_specs=[vm] * 2,
        scratch_shapes=[
            *[pltpu.VMEM(a.shape, a.dtype) for a in small],
            pltpu.VMEM((16, depth, width), bf16),
            pltpu.VMEM((toks, model), bf16),
            pltpu.VMEM((NE - 1, rows, model), bf16),
            pltpu.VMEM((toks + 16, chans), f32),
            pltpu.VMEM((16, chans), bf16),
            pltpu.VMEM((toks, chans), f32),
            pltpu.VMEM((toks, chans), f32),
            pltpu.VMEM((toks, chans), f32),
            pltpu.VMEM((2, n_state + 16, half), bf16),
            pltpu.VMEM((n_state + 16, half), bf16),
            pltpu.VMEM((NX, n_state + 16, half), bf16),
            pltpu.VMEM((n_state, half), bf16),
            pltpu.VMEM((2, n_state, half), bf16),
            pltpu.VMEM((2, n_state, half), bf16),
            pltpu.VMEM((n_state, half), bf16),
            pltpu.VMEM((toks, chans), bf16),
            dma((AG_SENDS + 8 * (NE - 1) + 7,)),
            dma((16, 4)),
            dma((NE - 1,)),
            dma((1 + NX,)),
            dma((3,)),
            dma((8,)),
        ],
        compiler_params=pltpu.CompilerParams(
            collective_id=1, has_side_effects=True, vmem_limit_bytes=56 * 2**20
        ),
        cost_estimate=pl.CostEstimate(
            flops=2 * toks * depth * model, bytes_accessed=20 * 2**20, transcendentals=0
        ),
        name="mixer",
    )(x_in, conv_w, b_proj, c_proj, log_decay, d_skip, w_out, gain)


def expert_kernel(
    nrm_ref, rt_ref, hid_ref, wr_ref, we_ref, out_ref,
    wv_ref, n_ref, r_ref, g_ref, a_ref, o_ref, sib_ref, yp_ref, yq_ref, xp_ref, xq_ref,
    con_ref, rec_ref, own_ref,
    lsem, ssem, nsem, tsem, gsem, bsem, psem, qsem, fsem, esem,
):
    w = Where()
    mail = Mail(ssem)
    rows, model = nrm_ref.shape
    cap = g_ref.shape[1]
    hidden = wv_ref.shape[2]
    toks = n_ref.shape[0]
    cut = model // 2
    P, Q = pl.ds(0, cut), pl.ds(cut, model - cut)
    loads = [pltpu.make_async_copy(we_ref.at[0, i], wv_ref.at[i], lsem.at[i]) for i in range(3)]
    for cp in loads:
        cp.start()
    lane = lax.broadcasted_iota(jnp.int32, (rows, 128), 1)
    ids = rt_ref[...].astype(f32)
    own_ref[...] = jnp.where(lane == 0, ids[:, 0:1], ids[:, 1:2]).astype(bf16)
    greet(w)

    def of(e):
        return pl.ds(pl.multiple_of(e * rows, rows), rows)

    me = of(w.e)
    for k in range(1, NE):
        mail.send(own_ref, r_ref.at[me], tsem.at[k - 1], {"expert": w.exp(k)})
    quarter = [pl.ds(i * (model // 4), model // 4) for i in range(4)]
    for i in (0, 2, 1, 3):
        for k in range(1, NE):
            mail.send(
                nrm_ref.at[:, quarter[i]], n_ref.at[me, quarter[i]], nsem.at[i, k - 1],
                {"expert": w.exp(k)},
            )
    n_ref[me, :] = nrm_ref[...]
    r_ref[me, :] = own_ref[...]
    for k in range(1, NE):
        mail.got(r_ref.at[of(w.exp(NE - k))], tsem.at[k - 1], {"expert": w.exp(k)})

    ii = lax.broadcasted_iota(jnp.int32, (toks, toks), 0)
    jj = lax.broadcasted_iota(jnp.int32, (toks, toks), 1)
    eye = (ii == jj).astype(f32)
    r1 = r_ref[:, 0:1].astype(f32)
    r2 = r_ref[:, 1:2].astype(f32)
    e_f = w.e.astype(f32)
    hit = jnp.where(r1 == e_f, 1.0, 0.0) + jnp.where(r2 == e_f, 1.0, 0.0)
    rank = jnp.sum(jnp.where(ii < jj, hit, 0.0), axis=0, keepdims=True)
    hit_row = jnp.sum(hit * eye, axis=0, keepdims=True)
    want = lax.broadcasted_iota(jnp.int32, (cap, toks), 0).astype(f32)
    sel_f = jnp.where(want == rank, 1.0, 0.0) * hit_row
    sel = sel_f.astype(bf16)

    def view(s, part):
        return g_ref.at[s, :, quarter[part]]

    ag = Gather(w, mail, view, gsem)

    def feed(i):
        cols = quarter[i]
        for k in range(1, NE):
            mail.got(n_ref.at[of(w.exp(NE - k)), cols], nsem.at[i, k - 1], {"expert": w.exp(k)})
        g_ref[0, :, cols] = jnp.dot(sel, n_ref[:, cols], preferred_element_type=f32).astype(bf16)
        ag.own(i)

    feed(0)
    feed(2)
    ag.arrive(1, 0, 0)
    ag.arrive(3, 0, 0)
    feed(1)
    ag.arrive(0, 1, 2)
    feed(3)

    logits = lax.dot_general(
        n_ref[...], wr_ref[...], (((1,), (1,)), ((), ())), preferred_element_type=f32
    )
    lane = lax.broadcasted_iota(jnp.int32, logits.shape, 1).astype(f32)
    s1 = jax.nn.sigmoid(jnp.sum(jnp.where(lane == r1, logits, 0.0), axis=1, keepdims=True))
    s2 = jax.nn.sigmoid(jnp.sum(jnp.where(lane == r2, logits, 0.0), axis=1, keepdims=True))
    gate = jnp.where(r1 == e_f, s1, s2) / (s1 + s2)
    gate_row = jnp.sum(gate * eye, axis=0, keepdims=True)
    gate_col = jnp.sum(sel_f * gate_row, axis=1, keepdims=True)

    def gate_up(group):
        xg = g_ref[pl.ds(group * 4, 4)].reshape(4 * cap, model)
        gv = jnp.dot(xg, wv_ref[0], preferred_element_type=f32)
        uv = jnp.dot(xg, wv_ref[1], preferred_element_type=f32)
        a_ref[...] = (gv / (1.0 + jnp.exp(-gv)) * uv).astype(bf16)

    def down(group):
        tile = 1024

        @pl.loop(0, model // tile)
        def _(i):
            cols = pl.ds(pl.multiple_of(i * tile, tile), tile)
            o = lax.dot_general(
                a_ref[...], wv_ref[2, cols, :], (((1,), (1,)), ((), ())), preferred_element_type=f32
            )
            o_ref[pl.ds(group * 4, 4), :, cols] = o.astype(bf16).reshape(4, cap, tile)

    def add(dst, cols, *srcs):
        @pl.loop(0, cap // 16)
        def _(i):
            r = pl.ds(pl.multiple_of(i * 16, 16), 16)
            v = o_ref[dst, r, cols].astype(f32)
            for src in srcs:
                v = v + src(r).astype(f32)
            o_ref[dst, r, cols] = v.astype(bf16)

    def pair_out(group):
        for p in (0, 1):
            i = group * 2 + p
            mail.send(o_ref.at[i * 2 + 1], sib_ref.at[i], bsem.at[i], w.tok_dev(0, 0, 1))

    def pair_in(group):
        for p in (0, 1):
            i = group * 2 + p
            dx, dy = ORDER[i]
            mail.got(sib_ref.at[i], bsem.at[i], w.tok_dev(0, 0, 1))
            add(i * 2, slice(None), lambda r, i=i: sib_ref[i, r, :])
            if dy == 1:
                mail.send(o_ref.at[i * 2, :, P], yp_ref.at[dx], psem.at[dx], w.tok_dev(0, 1, 0))
            if dx != 0:
                b = (NX - dx - 1) * 2 + dy
                mail.send(o_ref.at[i * 2, :, Q], xq_ref.at[b], qsem.at[b], w.tok_dev(dx, 0, 0))

    def y_sum(dx):
        mail.got(yp_ref.at[dx], psem.at[dx], w.tok_dev(0, 1, 0))
        add(slot(dx, 0, 0), P, lambda r: yp_ref[dx, r, :])
        if dx != 0:
            b = NX - dx - 1
            mail.send(o_ref.at[slot(dx, 0, 0), :, P], xp_ref.at[b], fsem.at[b], w.tok_dev(dx, 0, 0))

    def x_sum(dy):
        for b in range(3):
            mail.got(xq_ref.at[b * 2 + dy], qsem.at[b * 2 + dy], w.tok_dev(1, 0, 0))
        add(slot(0, dy, 0), Q, *[lambda r, b=b: xq_ref[b * 2 + dy, r, :] for b in range(3)])
        if dy == 1:
            mail.send(o_ref.at[slot(0, 1, 0), :, Q], yq_ref, fsem.at[3], w.tok_dev(0, 1, 0))

    for d in ((1, 0, 1), (3, 0, 1), (2, 0, 0), (0, 1, 3), (0, 1, 0), (0, 1, 1), (2, 0, 1)):
        ag.arrive(*d)
    ag.sib_in(0, 0)
    ag.sib_in(0, 1)
    loads[0].wait()
    loads[1].wait()
    gate_up(0)
    for part in (2, 3):
        ag.arrive(1, 0, part)
        ag.arrive(3, 0, part)
    loads[2].wait()
    down(0)
    pair_out(0)
    ag.sib_in(1, 0)
    ag.sib_in(3, 0)
    gate_up(1)
    for part in (2, 3):
        ag.arrive(1, 1, part)
        ag.arrive(3, 1, part)
        ag.arrive(2, 0, part)
    pair_in(0)
    down(1)
    pair_out(1)
    for part in (0, 1):
        ag.arrive(1, 1, part)
    ag.sib_in(2, 0)
    ag.sib_in(1, 1)
    gate_up(2)
    pair_in(1)
    for part in (0, 1):
        ag.arrive(3, 1, part)
    for part in (2, 3, 0, 1):
        ag.arrive(2, 1, part)
    down(2)
    pair_out(2)
    ag.sib_in(3, 1)
    ag.sib_in(2, 1)
    gate_up(3)
    pair_in(2)
    down(3)
    pair_out(3)
    y_sum(1)
    pair_in(3)
    x_sum(1)
    y_sum(3)
    y_sum(2)
    y_sum(0)
    x_sum(0)

    def final(i, cols, srcs):
        v = o_ref[0, :, cols].astype(f32)
        for src in srcs:
            v = v + src.astype(f32)
        con_ref[:, cols] = lax.dot_general(
            sel, (v * gate_col).astype(bf16), (((0,), (0,)), ((), ())), preferred_element_type=f32
        ).astype(bf16)
        for k in range(1, NE):
            mail.send(
                con_ref.at[of(w.exp(k)), cols], rec_ref.at[k - 1, :, cols], esem.at[i, k - 1],
                {"expert": w.exp(k)},
            )

    def finish(i, cols):
        total = hid_ref[:, cols].astype(f32) + con_ref[me, cols].astype(f32)
        for k in range(1, NE):
            mail.got(rec_ref.at[k - 1, :, cols], esem.at[i, k - 1], {"expert": w.exp(k)})
            total = total + rec_ref[k - 1, :, cols].astype(f32)
        out_ref[:, cols] = total.astype(bf16)

    mail.got(yq_ref, fsem.at[3], w.tok_dev(0, 1, 0))
    final(1, Q, [yq_ref[...]])
    for b in range(3):
        mail.got(xp_ref.at[b], fsem.at[b], w.tok_dev(1, 0, 0))
    final(0, P, [xp_ref[b] for b in range(3)])
    finish(1, Q)
    finish(0, P)
    mail.drain()


def expert_layer(normed, route, hidden, w_router, w_expert):
    rows, model = normed.shape
    units = w_expert.shape[3]
    toks, cap = rows * NE, 80
    cut = model // 2
    vm = pl.BlockSpec(memory_space=pltpu.VMEM)
    sends = 7 * (NE - 1) + AG_SENDS + 8 + 4 + 6 + 3 + 1
    dma = pltpu.SemaphoreType.DMA
    return pl.pallas_call(
        expert_kernel,
        out_shape=jax.ShapeDtypeStruct((rows, model), bf16),
        in_specs=[vm] * 4 + [pl.BlockSpec(memory_space=pl.ANY)],
        out_specs=vm,
        scratch_shapes=[
            pltpu.VMEM((3, model, units), bf16),
            pltpu.VMEM((toks, model), bf16),
            pltpu.VMEM((toks, 128), bf16),
            pltpu.VMEM((16, cap, model), bf16),
            pltpu.VMEM((4 * cap, units), bf16),
            pltpu.VMEM((16, cap, model), bf16),
            pltpu.VMEM((8, cap, model), bf16),
            pltpu.VMEM((4, cap, cut), bf16),
            pltpu.VMEM((cap, model - cut), bf16),
            pltpu.VMEM((3, cap, cut), bf16),
            pltpu.VMEM((6, cap, model - cut), bf16),
            pltpu.VMEM((toks, model), bf16),
            pltpu.VMEM((NE - 1, rows, model), bf16),
            pltpu.VMEM((rows, 128), bf16),
            dma((3,)), dma((sends,)), dma((4, NE - 1)), dma((NE - 1,)), dma((16, 4)), dma((8,)),
            dma((4,)), dma((6,)), dma((4,)), dma((2, NE - 1)),
        ],
        compiler_params=pltpu.CompilerParams(
            collective_id=2, has_side_effects=True, vmem_limit_bytes=60 * 2**20
        ),
        cost_estimate=pl.CostEstimate(
            flops=6 * 16 * cap * model * units, bytes_accessed=20 * 2**20, transcendentals=0
        ),
        name="expert_layer",
    )(normed, route, hidden, w_router, w_expert)


def on_device(
    x_in, conv_w, b_proj, c_proj, log_decay, d_skip, w_out, norm_gain, w_router, w_expert, route_ids
):
    rows, model = route_ids.shape[1], norm_gain.shape[0]
    hidden, normed = mixer(
        x_in, conv_w, b_proj, c_proj, log_decay.T, d_skip[None], w_out, norm_gain[None], rows
    )
    layer_out = expert_layer(normed, route_ids[0], hidden, w_router.T, w_expert)
    return layer_out.reshape(1, rows, model)


def solution(mesh):
    placed = (
        P("tok", "expert"),
        P(None, "expert"),
        P("tok", None),
        P("tok", None),
        P("tok", "expert"),
        P("expert"),
        P("expert", "tok"),
        P(),
        P(),
        P("expert", None, None, "tok"),
        P("tok", "expert", None),
    )
    return jax.shard_map(
        on_device, mesh=mesh, in_specs=placed, out_specs=P("tok", "expert", None), check_vma=False
    )
```

```python
import jax
import jax.numpy as jnp
from jax import lax
from jax.experimental import pallas as pl
from jax.experimental.pallas import tpu as pltpu
from jax.sharding import PartitionSpec as P

CONV = 4
HEAD = 64
highest = lax.Precision.HIGHEST
MESH = pl.DeviceIdType.MESH
bf16, f32 = jnp.bfloat16, jnp.float32
NX, NE = 4, 8
ORDER = [(0, 0), (0, 1), (1, 0), (3, 0), (2, 0), (2, 1), (1, 1), (3, 1)]
PLACE = {d: i for i, d in enumerate(ORDER)}


def slot(dx, dy, dc):
    return PLACE[(dx % NX, dy % 2)] * 2 + dc % 2


class Where:
    def __init__(self):
        self.e = lax.axis_index("expert")
        self.t = lax.axis_index("tok")
        self.c = lax.rem(self.t, 2)
        self.x = lax.rem(self.t // 2, NX)
        self.y = self.t // (2 * NX)

    def tok(self, dx, dy, dc):
        return (
            lax.rem(self.y + dy, 2) * NX + lax.rem(self.x + dx, NX)
        ) * 2 + lax.rem(self.c + dc, 2)

    def tok_dev(self, dx, dy, dc):
        return {"tok": self.tok(dx, dy, dc)}

    def exp(self, k):
        return lax.rem(self.e + k, NE)


NEAR = [(0, 0, 1), (0, 1, 0), (1, 0, 0), (3, 0, 0), (2, 0, 0)]


def greet(w, behind=False):
    barrier = pltpu.get_barrier_semaphore()
    for d in NEAR:
        pl.semaphore_signal(barrier, inc=1, device_id=w.tok_dev(*d), device_id_type=MESH)
    for k in range(1, NE):
        pl.semaphore_signal(barrier, inc=1, device_id={"expert": w.exp(k)}, device_id_type=MESH)
    if behind:
        back = lax.rem(w.t + 4 * NX - 1, 4 * NX)
        pl.semaphore_signal(barrier, inc=1, device_id={"tok": back}, device_id_type=MESH)
    pl.semaphore_wait(barrier, len(NEAR) + NE - 1 + behind)


class Mail:
    def __init__(self, sems):
        self.sems, self.out = sems, []

    def send(self, src, dst, rsem, dev):
        cp = pltpu.make_async_remote_copy(
            src_ref=src, dst_ref=dst, send_sem=self.sems.at[len(self.out)], recv_sem=rsem,
            device_id=dev, device_id_type=MESH,
        )
        cp.start()
        self.out.append(cp)

    def got(self, ref, rsem, dev):
        pltpu.make_async_remote_copy(
            src_ref=ref, dst_ref=ref, send_sem=self.sems.at[0], recv_sem=rsem,
            device_id=dev, device_id_type=MESH,
        ).wait_recv()

    def drain(self):
        for cp in self.out:
            cp.wait_send()


class Gather:
    def __init__(self, w, mail, view, rsems):
        self.w, self.mail, self.view, self.rsems = w, mail, view, rsems

    def put(self, frm, part, to, seen):
        s = slot(*seen)
        self.mail.send(
            self.view(slot(*frm), part), self.view(s, part), self.rsems.at[s, part],
            self.w.tok_dev(*to),
        )

    def got(self, dx, dy, dc, part):
        s = slot(dx, dy, dc)
        self.mail.got(self.view(s, part), self.rsems.at[s, part], self.w.tok_dev(0, 0, 1))

    def own_y(self, part):
        self.put((0, 0, 0), part, (0, 1, 0), (0, 1, 0))

    def own_sib(self, part):
        self.put((0, 0, 0), part, (0, 0, 1), (0, 0, 1))

    def along_x(self, dy, part):
        for dx in (1, 3):
            self.put((0, dy, 0), part, (dx, 0, 0), (-dx, dy, 0))

    def own(self, part):
        self.own_y(part)
        self.along_x(0, part)
        self.own_sib(part)

    def arrive(self, dx, dy, part):
        self.got(dx, dy, 0, part)
        on = (3, 1, 3, 1)[part]
        if dx == (NX - on) and (part > 1 or dy == 0):
            self.put((dx, dy, 0), part, (on, 0, 0), (2, dy, 0))
        if part < 2 and dx != 0 and dy == 0:
            self.put((dx, 0, 0), part, (0, 1, 0), (dx, 1, 0))
        if part > 1 and dx == 0:
            self.along_x(1, part)
        self.put((dx, dy, 0), part, (0, 0, 1), (dx, dy, 1))

    def sib_in(self, dx, dy):
        for part in range(4):
            self.got(dx, dy, 1, part)


AG_SENDS = 60


def rms(hid, gain):
    ms = jnp.mean(hid * hid, axis=-1, keepdims=True)
    return hid * lax.rsqrt(ms + 1e-05) * gain


def mixer_kernel(
    x_hbm, cw_hbm, b_hbm, c_hbm, ld_hbm, ds_hbm, wout_ref, gain_hbm,
    hid_ref, nrm_ref,
    x_ref, cw_ref, b_ref, c_ref, ld_ref, ds_ref, gain_ref,
    g_ref, part_ref, rec_ref, ext_ref, tail_ref, conv_ref, y_ref, ent_ref, st_ref, s1_ref, s2_ref,
    r_in_ref, r_out_ref, sin_ref, hand_ref, scan_ref,
    ssem, rsem, esem, tsem, usem, lsem,
):
    w = Where()
    mail = Mail(ssem)
    loads = [
        pltpu.make_async_copy(src, dst, lsem.at[i])
        for i, (src, dst) in enumerate((
            (x_hbm, x_ref), (wout_ref, g_ref.at[0]), (cw_hbm, cw_ref), (ld_hbm, ld_ref),
            (b_hbm, b_ref), (c_hbm, c_ref), (ds_hbm, ds_ref), (gain_hbm, gain_ref),
        ))
    ]
    for cp in loads:
        cp.start()
    toks, chans = x_ref.shape
    heads = ld_ref.shape[0]
    half = chans // 2
    n_state = b_ref.shape[1]
    depth, width = wout_ref.shape
    cut = depth // 4
    sib = w.tok_dev(0, 0, 1)
    greet(w, behind=True)
    loads[0].wait()
    mail.send(
        x_ref.at[pl.ds(toks - 16, 16)], tail_ref, tsem.at[0], {"tok": lax.rem(w.t + 1, 4 * NX)}
    )

    def view(s, part):
        return g_ref.at[s, pl.ds(part * cut, cut)]

    ag = Gather(w, mail, view, rsem)
    loads[1].wait()
    for part in (0, 1):
        ag.along_x(0, part)
    for part in (2, 0, 3, 1):
        ag.own_y(part)
    for cp in loads[2:]:
        cp.wait()

    ext_ref[16:, :] = x_ref[...].astype(f32)
    mail.got(tail_ref, tsem.at[0], sib)
    ext_ref[0:16, :] = jnp.where(w.t > 0, tail_ref[...].astype(f32), 0.0)
    for b in range(chans // 256):
        cols = pl.ds(b * 256, 256)
        v = cw_ref[0:1, cols] * ext_ref[13 : 13 + toks, cols]
        for k in range(1, CONV):
            v = v + cw_ref[k : k + 1, cols] * ext_ref[13 + k : 13 + k + toks, cols]
        conv_ref[:, cols] = v / (1.0 + jnp.exp(-v))

    ii = lax.broadcasted_iota(jnp.int32, (toks, toks), 0)
    jj = lax.broadcasted_iota(jnp.int32, (toks, toks), 1)
    low = ii >= jj
    lowf = jnp.where(low, 1.0, 0.0)
    cum = lax.dot_general(
        lowf, ld_ref[...], (((1,), (1,)), ((), ())),
        precision=highest, preferred_element_type=f32,
    )
    cum_t = jnp.dot(
        ld_ref[...], jnp.where(ii <= jj, 1.0, 0.0), precision=highest, preferred_element_type=f32
    )
    eh = lax.broadcasted_iota(jnp.int32, (heads, chans), 0) * HEAD
    ec = lax.broadcasted_iota(jnp.int32, (heads, chans), 1)
    spread = jnp.where((ec >= eh) & (ec < eh + HEAD), 1.0, 0.0)
    both = jnp.concatenate([cum, cum[toks - 1 : toks] - cum], axis=0)
    skip = jnp.dot(ds_ref[...], spread, precision=highest, preferred_element_type=f32)
    for h in range(2):
        for b in range(2):
            cols = pl.ds(h * half + b * (half // 2), half // 2)
            here = pl.ds(b * (half // 2), half // 2)
            sp = spread[:, h * half + b * (half // 2) : h * half + (b + 1) * (half // 2)]
            lev = jnp.exp(jnp.dot(both, sp, precision=highest, preferred_element_type=f32))
            ent_ref[:, cols] = lev[:toks]
            total = lev[toks - 1 : toks]
            xw = (conv_ref[:, cols] * lev[toks:]).astype(bf16)
            st_ref[h, 0:n_state, here] = lax.dot_general(
                b_ref[...], xw, (((0,), (0,)), ((), ())), preferred_element_type=f32
            ).astype(bf16)
            hi = total.astype(bf16).astype(f32)
            row = lax.broadcasted_iota(jnp.int32, (16, half // 2), 0)
            st_ref[h, n_state : n_state + 16, here] = jnp.where(row == 0, hi, total - hi).astype(bf16)

    mail.send(st_ref.at[1 - w.c], s1_ref, usem.at[0], sib)

    scores = lax.dot_general(
        c_ref[...], b_ref[...], (((1,), (1,)), ((), ())), preferred_element_type=f32
    )
    scores = jnp.where(low, scores, 0.0)
    lane = lax.broadcasted_iota(jnp.int32, (toks, 2 * HEAD), 1)

    def inside(p):
        cols = pl.ds(p * 2 * HEAD, 2 * HEAD)
        xc = conv_ref[:, cols]
        mats = []
        for h in (2 * p, 2 * p + 1):
            gap = jnp.where(low, cum[:, h : h + 1] - cum_t[h : h + 1, :], 0.0)
            mats.append((jnp.exp(gap) * scores).astype(bf16))
        yy = jnp.dot(jnp.concatenate(mats, axis=0), xc.astype(bf16), preferred_element_type=f32)
        y_ref[:, cols] = (
            jnp.where(lane < HEAD, yy[:toks], yy[toks:])
            + skip[:, p * 2 * HEAD : (p + 1) * 2 * HEAD] * xc
        )

    for p in range(2):
        inside(p)

    def by_rows(body):
        @pl.loop(0, n_state // 16)
        def _(i):
            body(pl.ds(pl.multiple_of(i * 16, 16), 16))

    def decay_of(block):
        v = block.astype(f32)
        return v[0:1] + v[1:2]

    DEC = pl.ds(n_state, 16)
    mail.got(s1_ref, usem.at[0], sib)
    own_d = decay_of(st_ref[w.c, DEC, :])
    sib_d = decay_of(s1_ref[DEC, :])
    first = w.c == 0
    d0 = jnp.where(first, own_d, sib_d)
    d1 = jnp.where(first, sib_d, own_d)
    chip_d = d0 * d1
    chip_hi = chip_d.astype(bf16).astype(f32)
    row = lax.broadcasted_iota(jnp.int32, (16, half), 0)
    s2_ref[w.x, DEC, :] = jnp.where(row == 0, chip_hi, chip_d - chip_hi).astype(bf16)

    def join(r):
        own, other = st_ref[w.c, r, :].astype(f32), s1_ref[r, :].astype(f32)
        s2_ref[w.x, r, :] = (
            d1 * jnp.where(first, own, other) + jnp.where(first, other, own)
        ).astype(bf16)

    by_rows(join)
    for i, dx in enumerate((1, 3, 2)):
        mail.send(s2_ref.at[w.x], s2_ref.at[w.x], tsem.at[1 + NX - dx], w.tok_dev(dx, 0, 0))
    for part in (2, 3):
        ag.along_x(0, part)
    for part in range(4):
        ag.own_sib(part)
    for p in range(2, heads // 2):
        inside(p)
    for d in ((1, 0, 0), (3, 0, 0), (0, 1, 2)):
        ag.arrive(*d)
    for dx in (1, 3, 2):
        mail.got(s2_ref.at[lax.rem(w.x + dx, NX)], tsem.at[1 + dx], w.tok_dev(dx, 0, 0))
    decs = [decay_of(s2_ref[k, DEC, :]) for k in range(NX)]
    before_d = jnp.ones_like(chip_d)
    for k in range(NX):
        before_d = before_d * jnp.where(w.x > k, decs[k], 1.0)

    def row_scan(r):
        run = jnp.zeros((16, half), f32)
        before = run
        for k in range(NX):
            before = jnp.where(w.x == k, run, before)
            run = decs[k] * run + s2_ref[k, r, :].astype(f32)
        r_out_ref[0, r, :] = run.astype(bf16)
        r_out_ref[1, r, :] = before.astype(bf16)

    by_rows(row_scan)
    mail.send(r_out_ref.at[0], r_in_ref, usem.at[1], w.tok_dev(0, 1, 0))
    for d in ((1, 0, 1), (3, 0, 1), (0, 1, 3), (0, 1, 0), (0, 1, 1), (2, 0, 0), (2, 0, 1)):
        ag.arrive(*d)
    mail.got(r_in_ref, usem.at[1], w.tok_dev(0, 1, 0))
    lower = w.y > 0

    def enter(r):
        chip = r_out_ref[1, r, :].astype(f32) + jnp.where(
            lower, before_d * r_in_ref[r, :].astype(f32), 0.0
        )
        s0 = jnp.where(first, st_ref[w.c, r, :], s1_ref[r, :]).astype(f32)
        second = d0 * chip + s0
        sin_ref[w.c, r, :] = jnp.where(first, chip, second).astype(bf16)
        hand_ref[r, :] = jnp.where(first, second, chip).astype(bf16)

    by_rows(enter)
    mail.send(hand_ref, sin_ref.at[w.c], usem.at[2], sib)

    for part in (2, 3):
        for d in ((1, 0, part), (3, 0, part)):
            ag.arrive(*d)

    def close(h):
        for b in range(2):
            cols = pl.ds(pl.multiple_of(h * half + b * (half // 2), half // 2), half // 2)
            here = pl.ds(b * (half // 2), half // 2)
            carry = jnp.dot(c_ref[...], sin_ref[h, :, here], preferred_element_type=f32)
            scan_ref[:, cols] = (y_ref[:, cols] + ent_ref[:, cols] * carry).astype(bf16)

    close(w.c)
    mail.got(sin_ref.at[1 - w.c], usem.at[2], sib)
    close(1 - w.c)

    def mult(dx, dy, dc):
        cols = pl.ds(pl.multiple_of(w.tok(dx, dy, dc) * width, width), width)
        part_ref[:, cols] = jnp.dot(
            scan_ref[...], g_ref[slot(dx, dy, dc)], preferred_element_type=f32
        ).astype(bf16)

    rows = hid_ref.shape[0]

    def mine(e):
        return pl.ds(pl.multiple_of(e * rows, rows), rows)

    def out(dx, dy):
        chip = (w.tok(dx, dy, 0) // 2) * 2 * width
        cols = pl.ds(pl.multiple_of(chip, 2 * width), 2 * width)
        for k in range(1, NE):
            mail.send(
                part_ref.at[mine(w.exp(k)), cols], rec_ref.at[k - 1, :, cols], esem.at[k - 1],
                {"expert": w.exp(k)},
            )

    def pair(dx, dy):
        mult(dx, dy, 0)
        ag.sib_in(dx, dy)
        mult(dx, dy, 1)
        out(dx, dy)

    for part in (2, 3):
        for d in ((1, 1, part), (3, 1, part), (2, 0, part)):
            ag.arrive(*d)
    for d in ((0, 0), (0, 1), (1, 0), (3, 0), (2, 0)):
        pair(*d)
    for dx in (1, 3):
        for part in (0, 1):
            ag.arrive(dx, 1, part)
        pair(dx, 1)
    for part in (2, 3, 0, 1):
        ag.arrive(2, 1, part)
    pair(2, 1)
    total = part_ref[mine(w.e), :].astype(f32)
    for k in range(1, NE):
        mail.got(rec_ref.at[k - 1], esem.at[k - 1], {"expert": w.exp(k)})
        total = total + rec_ref[k - 1].astype(f32)
    hid_b = total.astype(bf16)
    hid_ref[...] = hid_b
    nrm_ref[...] = rms(hid_b.astype(f32), gain_ref[...]).astype(bf16)
    mail.drain()


def mixer(x_in, conv_w, b_proj, c_proj, log_decay, d_skip, w_out, gain, rows):
    depth, width = w_out.shape
    toks, chans = x_in.shape
    model, n_state = gain.shape[1], b_proj.shape[1]
    half = chans // 2
    small = (x_in, conv_w, b_proj, c_proj, log_decay, d_skip, gain)
    vm = pl.BlockSpec(memory_space=pltpu.VMEM)
    dma = pltpu.SemaphoreType.DMA
    return pl.pallas_call(
        mixer_kernel,
        out_shape=[jax.ShapeDtypeStruct((rows, model), bf16)] * 2,
        in_specs=[pl.BlockSpec(memory_space=pl.ANY)] * 8,
        out_specs=[vm] * 2,
        scratch_shapes=[
            *[pltpu.VMEM(a.shape, a.dtype) for a in small],
            pltpu.VMEM((16, depth, width), bf16),
            pltpu.VMEM((toks, model), bf16),
            pltpu.VMEM((NE - 1, rows, model), bf16),
            pltpu.VMEM((toks + 16, chans), f32),
            pltpu.VMEM((16, chans), bf16),
            pltpu.VMEM((toks, chans), f32),
            pltpu.VMEM((toks, chans), f32),
            pltpu.VMEM((toks, chans), f32),
            pltpu.VMEM((2, n_state + 16, half), bf16),
            pltpu.VMEM((n_state + 16, half), bf16),
            pltpu.VMEM((NX, n_state + 16, half), bf16),
            pltpu.VMEM((n_state, half), bf16),
            pltpu.VMEM((2, n_state, half), bf16),
            pltpu.VMEM((2, n_state, half), bf16),
            pltpu.VMEM((n_state, half), bf16),
            pltpu.VMEM((toks, chans), bf16),
            dma((AG_SENDS + 8 * (NE - 1) + 7,)),
            dma((16, 4)),
            dma((NE - 1,)),
            dma((1 + NX,)),
            dma((3,)),
            dma((8,)),
        ],
        compiler_params=pltpu.CompilerParams(
            collective_id=1, has_side_effects=True, vmem_limit_bytes=56 * 2**20
        ),
        cost_estimate=pl.CostEstimate(
            flops=2 * toks * depth * model, bytes_accessed=20 * 2**20, transcendentals=0
        ),
        name="mixer",
    )(x_in, conv_w, b_proj, c_proj, log_decay, d_skip, w_out, gain)


def expert_kernel(
    nrm_ref, rt_ref, hid_ref, wr_ref, we_ref, out_ref,
    wv_ref, n_ref, r_ref, g_ref, a_ref, o_ref, sib_ref, yp_ref, yq_ref, xf_ref, xr_ref, sum_ref,
    con_ref, rec_ref, own_ref,
    lsem, ssem, nsem, tsem, gsem, bsem, psem, qsem, rsem, fsem, esem,
):
    w = Where()
    mail = Mail(ssem)
    rows, model = nrm_ref.shape
    cap = g_ref.shape[1]
    hidden = wv_ref.shape[2]
    toks = n_ref.shape[0]
    cut = model // 2
    P, Q = pl.ds(0, cut), pl.ds(cut, model - cut)
    loads = [pltpu.make_async_copy(we_ref.at[0, i], wv_ref.at[i], lsem.at[i]) for i in range(3)]
    for cp in loads:
        cp.start()
    lane = lax.broadcasted_iota(jnp.int32, (rows, 128), 1)
    ids = rt_ref[...].astype(f32)
    same = lax.broadcasted_iota(jnp.int32, (rows, rows), 0) == lax.broadcasted_iota(
        jnp.int32, (rows, rows), 1
    )
    cols = [
        jnp.sum(jnp.where(same, ids[k : k + 1, :], 0.0), axis=1, keepdims=True) for k in (0, 1)
    ]
    own_ref[...] = jnp.where(lane == 0, cols[0], cols[1]).astype(bf16)
    greet(w)

    def of(e):
        return pl.ds(pl.multiple_of(e * rows, rows), rows)

    me = of(w.e)
    for k in range(1, NE):
        mail.send(own_ref, r_ref.at[me], tsem.at[k - 1], {"expert": w.exp(k)})
    quarter = [pl.ds(i * (model // 4), model // 4) for i in range(4)]
    for i in (0, 2, 1, 3):
        for k in range(1, NE):
            mail.send(
                nrm_ref.at[:, quarter[i]], n_ref.at[me, quarter[i]], nsem.at[i, k - 1],
                {"expert": w.exp(k)},
            )
    n_ref[me, :] = nrm_ref[...]
    r_ref[me, :] = own_ref[...]
    for k in range(1, NE):
        mail.got(r_ref.at[of(w.exp(NE - k))], tsem.at[k - 1], {"expert": w.exp(k)})

    ii = lax.broadcasted_iota(jnp.int32, (toks, toks), 0)
    jj = lax.broadcasted_iota(jnp.int32, (toks, toks), 1)
    eye = (ii == jj).astype(f32)
    r1 = r_ref[:, 0:1].astype(f32)
    r2 = r_ref[:, 1:2].astype(f32)
    e_f = w.e.astype(f32)
    hit = jnp.where(r1 == e_f, 1.0, 0.0) + jnp.where(r2 == e_f, 1.0, 0.0)
    rank = jnp.sum(jnp.where(ii < jj, hit, 0.0), axis=0, keepdims=True)
    hit_row = jnp.sum(hit * eye, axis=0, keepdims=True)
    want = lax.broadcasted_iota(jnp.int32, (cap, toks), 0).astype(f32)
    sel_f = jnp.where(want == rank, 1.0, 0.0) * hit_row
    sel = sel_f.astype(bf16)

    def view(s, part):
        return g_ref.at[s, :, quarter[part]]

    ag = Gather(w, mail, view, gsem)

    def feed(i):
        cols = quarter[i]
        for k in range(1, NE):
            mail.got(n_ref.at[of(w.exp(NE - k)), cols], nsem.at[i, k - 1], {"expert": w.exp(k)})
        g_ref[0, :, cols] = jnp.dot(sel, n_ref[:, cols], preferred_element_type=f32).astype(bf16)
        ag.own(i)

    feed(0)
    feed(2)
    ag.arrive(1, 0, 0)
    ag.arrive(3, 0, 0)
    feed(1)
    ag.arrive(0, 1, 2)
    feed(3)

    logits = lax.dot_general(
        n_ref[...], wr_ref[...], (((1,), (1,)), ((), ())), preferred_element_type=f32
    )
    lane = lax.broadcasted_iota(jnp.int32, logits.shape, 1).astype(f32)
    s1 = jax.nn.sigmoid(jnp.sum(jnp.where(lane == r1, logits, 0.0), axis=1, keepdims=True))
    s2 = jax.nn.sigmoid(jnp.sum(jnp.where(lane == r2, logits, 0.0), axis=1, keepdims=True))
    gate = jnp.where(r1 == e_f, s1, s2) / (s1 + s2)
    gate_row = jnp.sum(gate * eye, axis=0, keepdims=True)
    gate_col = jnp.sum(sel_f * gate_row, axis=1, keepdims=True)

    def gate_up(group):
        xg = g_ref[pl.ds(group * 4, 4)].reshape(4 * cap, model)
        gv = jnp.dot(xg, wv_ref[0], preferred_element_type=f32)
        uv = jnp.dot(xg, wv_ref[1], preferred_element_type=f32)
        a_ref[...] = (gv / (1.0 + jnp.exp(-gv)) * uv).astype(bf16)

    def down(group):
        tile = 1024

        @pl.loop(0, model // tile)
        def _(i):
            cols = pl.ds(pl.multiple_of(i * tile, tile), tile)
            o = lax.dot_general(
                a_ref[...], wv_ref[2, cols, :], (((1,), (1,)), ((), ())), preferred_element_type=f32
            )
            o_ref[pl.ds(group * 4, 4), :, cols] = o.astype(bf16).reshape(4, cap, tile)

    def add(dst, cols, *srcs, out=None):
        @pl.loop(0, cap // 16)
        def _(i):
            r = pl.ds(pl.multiple_of(i * 16, 16), 16)
            v = o_ref[dst, r, cols].astype(f32)
            for src in srcs:
                v = v + src(r).astype(f32)
            if out is None:
                o_ref[dst, r, cols] = v.astype(bf16)
            else:
                out[r, :] = v

    def pair_out(group):
        for p in (0, 1):
            i = group * 2 + p
            mail.send(o_ref.at[i * 2 + 1], sib_ref.at[i], bsem.at[i], w.tok_dev(0, 0, 1))

    def pair_in(group):
        for p in (0, 1):
            i = group * 2 + p
            dx, dy = ORDER[i]
            mail.got(sib_ref.at[i], bsem.at[i], w.tok_dev(0, 0, 1))
            add(i * 2, slice(None), lambda r, i=i: sib_ref[i, r, :])
            if dy == 1:
                mail.send(o_ref.at[i * 2, :, P], yp_ref.at[dx], psem.at[dx], w.tok_dev(0, 1, 0))
            spread(dx, dy, 2)

    def lot(dy, part):
        return (dy if part > 1 else 2) * 2 + part % 2

    def pass_on(dx, dy, part, to, relayed=False):
        i = lot(dy, part)
        if relayed:
            dst, sem = xr_ref.at[i], rsem.at[i]
        else:
            side = 0 if to == 1 else 1
            dst, sem = xf_ref.at[i * 2 + side], qsem.at[i * 2 + side]
        mail.send(o_ref.at[slot(dx, dy, 0), :, quarter[part]], dst, sem, w.tok_dev(to, 0, 0))

    def spread(dx, dy, part):
        if dx == 2:
            pass_on(2, dy, part, 1, True)
            pass_on(2, dy, part + 1, 3, True)
        if dx == 1:
            pass_on(1, dy, part + 1, 1)
        if dx == 3:
            pass_on(3, dy, part, 3)

    def relay(dy, part):
        for p, to in ((part, 1), (part + 1, 3)):
            i = lot(dy, p)
            mail.got(xr_ref.at[i], rsem.at[i], w.tok_dev(1, 0, 0))
            add(slot(to, dy, 0), quarter[p], lambda r, i=i: xr_ref[i, r, :])
            pass_on(to, dy, p, to)

    def x_in(dy, part):
        for p in (part, part + 1):
            for side in (0, 1):
                i = lot(dy, p) * 2 + side
                mail.got(xf_ref.at[i], qsem.at[i], w.tok_dev(1, 0, 0))

    def y_sum(dx):
        mail.got(yp_ref.at[dx], psem.at[dx], w.tok_dev(0, 1, 0))
        add(slot(dx, 0, 0), P, lambda r: yp_ref[dx, r, :])
        spread(dx, 0, 0)

    def x_sum(dy):
        x_in(dy, 2)
        for p in (2, 3):
            i = lot(dy, p) * 2
            add(
                slot(0, dy, 0), quarter[p],
                lambda r, i=i: xf_ref[i, r, :], lambda r, i=i: xf_ref[i + 1, r, :],
            )
        if dy == 1:
            mail.send(o_ref.at[slot(0, 1, 0), :, Q], yq_ref, fsem.at[0], w.tok_dev(0, 1, 0))

    for d in ((1, 0, 1), (3, 0, 1), (2, 0, 0), (0, 1, 3), (0, 1, 0), (0, 1, 1), (2, 0, 1)):
        ag.arrive(*d)
    ag.sib_in(0, 0)
    ag.sib_in(0, 1)
    loads[0].wait()
    loads[1].wait()
    gate_up(0)
    for part in (2, 3):
        ag.arrive(1, 0, part)
        ag.arrive(3, 0, part)
    loads[2].wait()
    down(0)
    pair_out(0)
    ag.sib_in(1, 0)
    ag.sib_in(3, 0)
    gate_up(1)
    for part in (2, 3):
        ag.arrive(1, 1, part)
        ag.arrive(3, 1, part)
        ag.arrive(2, 0, part)
    pair_in(0)
    down(1)
    pair_out(1)
    for part in (0, 1):
        ag.arrive(1, 1, part)
        ag.arrive(3, 1, part)
    for part in (2, 3, 0, 1):
        ag.arrive(2, 1, part)
    ag.sib_in(2, 0)
    ag.sib_in(2, 1)
    gate_up(2)
    pair_in(1)
    down(2)
    pair_out(2)
    ag.sib_in(1, 1)
    ag.sib_in(3, 1)
    gate_up(3)
    pair_in(2)
    down(3)
    pair_out(3)
    relay(0, 2)
    pair_in(3)
    relay(1, 2)
    y_sum(2)
    x_sum(1)
    y_sum(1)
    y_sum(3)
    relay(0, 0)
    y_sum(0)
    x_sum(0)

    def final(i, cols, srcs):
        if srcs is None:
            v = jnp.concatenate([sum_ref[0], sum_ref[1]], axis=1)
        else:
            v = o_ref[0, :, cols].astype(f32)
            for src in srcs:
                v = v + src.astype(f32)
        con_ref[:, cols] = lax.dot_general(
            sel, (v * gate_col).astype(bf16), (((0,), (0,)), ((), ())), preferred_element_type=f32
        ).astype(bf16)
        for k in range(1, NE):
            mail.send(
                con_ref.at[of(w.exp(k)), cols], rec_ref.at[k - 1, :, cols], esem.at[i, k - 1],
                {"expert": w.exp(k)},
            )

    def finish(i, cols):
        total = hid_ref[:, cols].astype(f32) + con_ref[me, cols].astype(f32)
        for k in range(1, NE):
            mail.got(rec_ref.at[k - 1, :, cols], esem.at[i, k - 1], {"expert": w.exp(k)})
            total = total + rec_ref[k - 1, :, cols].astype(f32)
        out_ref[:, cols] = total.astype(bf16)

    mail.got(yq_ref, fsem.at[0], w.tok_dev(0, 1, 0))
    final(1, Q, [yq_ref[...]])
    x_in(0, 0)
    for p in (0, 1):
        i = lot(0, p) * 2
        add(
            0, quarter[p], lambda r, i=i: xf_ref[i, r, :], lambda r, i=i: xf_ref[i + 1, r, :],
            out=sum_ref.at[p],
        )
    final(0, P, None)
    finish(1, Q)
    finish(0, P)
    mail.drain()


def expert_layer(normed, route, hidden, w_router, w_expert):
    rows, model = normed.shape
    units = w_expert.shape[3]
    toks, cap = rows * NE, 80
    cut = model // 2
    vm = pl.BlockSpec(memory_space=pltpu.VMEM)
    sends = 7 * (NE - 1) + AG_SENDS + 8 + 4 + 12 + 1 + 6
    dma = pltpu.SemaphoreType.DMA
    return pl.pallas_call(
        expert_kernel,
        out_shape=jax.ShapeDtypeStruct((rows, model), bf16),
        in_specs=[vm] * 4 + [pl.BlockSpec(memory_space=pl.ANY)],
        out_specs=vm,
        scratch_shapes=[
            pltpu.VMEM((3, model, units), bf16),
            pltpu.VMEM((toks, model), bf16),
            pltpu.VMEM((toks, 128), bf16),
            pltpu.VMEM((16, cap, model), bf16),
            pltpu.VMEM((4 * cap, units), bf16),
            pltpu.VMEM((16, cap, model), bf16),
            pltpu.VMEM((8, cap, model), bf16),
            pltpu.VMEM((4, cap, cut), bf16),
            pltpu.VMEM((cap, model - cut), bf16),
            pltpu.VMEM((12, cap, model // 4), bf16),
            pltpu.VMEM((6, cap, model // 4), bf16),
            pltpu.VMEM((2, cap, model // 4), f32),
            pltpu.VMEM((toks, model), bf16),
            pltpu.VMEM((NE - 1, rows, model), bf16),
            pltpu.VMEM((rows, 128), bf16),
            dma((3,)), dma((sends,)), dma((4, NE - 1)), dma((NE - 1,)), dma((16, 4)), dma((8,)),
            dma((4,)), dma((12,)), dma((6,)), dma((1,)), dma((2, NE - 1)),
        ],
        compiler_params=pltpu.CompilerParams(
            collective_id=2, has_side_effects=True, vmem_limit_bytes=60 * 2**20
        ),
        cost_estimate=pl.CostEstimate(
            flops=6 * 16 * cap * model * units, bytes_accessed=20 * 2**20, transcendentals=0
        ),
        name="expert_layer",
    )(normed, route, hidden, w_router, w_expert)


def on_device(
    x_in, conv_w, b_proj, c_proj, log_decay, d_skip, w_out, norm_gain, w_router, w_expert, route_ids
):
    rows, model = route_ids.shape[1], norm_gain.shape[0]
    hidden, normed = mixer(
        x_in, conv_w, b_proj, c_proj, log_decay.T, d_skip[None], w_out, norm_gain[None], rows
    )
    layer_out = expert_layer(normed, route_ids[0].T, hidden, w_router.T, w_expert)
    return layer_out.reshape(1, rows, model)


def solution(mesh):
    placed = (
        P("tok", "expert"),
        P(None, "expert"),
        P("tok", None),
        P("tok", None),
        P("tok", "expert"),
        P("expert"),
        P("expert", "tok"),
        P(),
        P(),
        P("expert", None, None, "tok"),
        P("tok", "expert", None),
    )
    return jax.shard_map(
        on_device, mesh=mesh, in_specs=placed, out_specs=P("tok", "expert", None), check_vma=False
    )
```
